128 devices in a mesh: row: 8 (over x, core), col: 16 (over y, z).
Axes of the slice: x: 4, y: 4, z: 4, core: 2. Of those that a mesh axis runs over, the one named last changes fastest.
Arguments:
- object_field: float32 [2, 4096, 8192], P(None, 'row', 'col'), may hold values from -5 to 5
- probe_field: float32 [2, 256, 256], replicated, may hold values from -6 to 6
- measured: float32 [2048, 256, 256], P(('row', 'col')), may hold values from 0 to 2
- positions: int32 [2048, 2], P(('row', 'col')), may hold values from 0 to 7936, as said below
- counts: int32 [128], replicated, may hold values from 1 to 16, as said below
Outputs:
- new_object: float32 [2, 4096, 8192], P(None, 'row', 'col')
- new_probe: float32 [2, 256, 256], replicated
The draws below stay inside these ranges and needn't reach their ends.
Inputs may be any that keep to these rules, and one draw needn't show every extreme that they name: `positions`: each slot's window lies whole in the object, and its top-left cell lies in the tile of the device that holds the slot (tiles of 512 x 512 cells in row-major device order). `counts`: some device's bucket is full.
All inputs are finite; a program needn't handle non-finite values.
Results may differ from the reference program's by a relative error of at most 0.0003.
Values sent between devices are 32-bit elements; how exact they have to be, the bound alone decides.
No kernel may reach another device: no remote copies, remote signals or barrier semaphores. Data moves between devices by JAX's collectives and lax.ppermute only.
A program may use at most 128 MiB of HBM per device.

```python
import jax
import jax.numpy as jnp
from jax import lax

PIX = 256
TR = 512
TC = 512
PAT_DEV = 16
NY = 4096
NX = 8192
NPAT = 2048


def draw_counts(key, part):
    key = jax.random.fold_in(key, 11)
    device_total = NY // TR * (NX // TC)
    levels = jax.random.randint(jax.random.fold_in(key, 1), (device_total,), 0, 4)
    filled = jnp.right_shift(jnp.full((device_total,), PAT_DEV, jnp.int32), levels.astype(jnp.int32))
    filled = jnp.maximum(filled, 1)
    chosen = jax.random.randint(jax.random.fold_in(key, 2), (), 0, device_total)
    device_ids = jnp.arange(device_total, dtype=jnp.int32)
    return jnp.where(device_ids == chosen, PAT_DEV, filled).astype(jnp.int32)


def draw_positions(key, part):
    key = jax.random.fold_in(key, 23)
    slot_total = PAT_DEV * (NY // TR) * (NX // TC)
    col_count = NX // TC
    slot_ids = jnp.arange(slot_total, dtype=jnp.int32)
    device_ids = slot_ids // PAT_DEV
    row_base = device_ids // col_count * TR
    col_base = device_ids % col_count * TC
    row_span = jnp.minimum(row_base + TR, NY - PIX + 1) - row_base
    col_span = jnp.minimum(col_base + TC, NX - PIX + 1) - col_base
    row_draw = jax.random.randint(jax.random.fold_in(key, 1), (slot_total,), 0, 1 << 20)
    col_draw = jax.random.randint(jax.random.fold_in(key, 2), (slot_total,), 0, 1 << 20)
    top_rows = row_base + row_draw % row_span
    left_cols = col_base + col_draw % col_span
    return jnp.stack([top_rows, left_cols], axis=1).astype(jnp.int32)


def shard_levels(key, dims, split, least, largest):
    level = 1.0
    for dim, shards_of in split:
        heights = jax.random.uniform(jax.random.fold_in(jax.random.fold_in(key, 6), dim), (shards_of,), jnp.float32, least / len(split), largest / len(split))
        level = level * jnp.repeat(jnp.exp(heights), dims[dim] // shards_of).reshape((-1,) + (1,) * (len(dims) - 1 - dim))
    return level


def scatter_about(key, dims, scale, limit, shards=(), kind=jnp.bfloat16):
    array = jax.random.normal(key, dims, jnp.float32) * scale
    if len(shards) > 0:
        array = shard_levels(key, dims, shards, -0.22, 0.18) * array
    return jnp.clip(array, min=-limit, max=limit).astype(kind)


def setup_inputs(seed: int = 0) -> dict:
    streams_of = jax.random.split(jax.random.key(seed), 6)
    object_field = scatter_about(streams_of[0], (2, NY, NX), 0.7, 5.0, ((1, 8), (2, 16)), jnp.float32)
    probe_field = scatter_about(streams_of[1], (2, PIX, PIX), 1.0, 6.0, (), jnp.float32)
    measured = jnp.clip(2.0 * jax.random.uniform(streams_of[2], (NPAT, PIX, PIX), jnp.float32) ** shard_levels(streams_of[2], (NPAT, PIX, PIX), ((0, 128),), -0.2, 0.2), 0.0, 2.0)
    positions = draw_positions(jax.random.fold_in(streams_of[5], 71), 0)
    counts = draw_counts(jax.random.fold_in(streams_of[5], 71), 0)
    return dict(object_field=object_field, probe_field=probe_field, measured=measured, positions=positions, counts=counts)


AMPLITUDE_FLOOR = 0.25
OBJECT_RATE = 0.5

def exit_update(object_patch, probe_field, amplitude):
    probe_re, probe_im = (probe_field[0], probe_field[1])
    patch_re, patch_im = (object_patch[0], object_patch[1])
    exit_re = probe_re * patch_re - probe_im * patch_im
    exit_im = probe_re * patch_im + probe_im * patch_re
    spectrum = jnp.fft.fft2(lax.complex(exit_re, exit_im), norm='ortho')
    spec_re = jnp.real(spectrum)
    spec_im = jnp.imag(spectrum)
    magnitude = jnp.sqrt(spec_re * spec_re + spec_im * spec_im)
    factor = amplitude / jnp.maximum(magnitude, AMPLITUDE_FLOOR)
    returned = jnp.fft.ifft2(lax.complex(spec_re * factor, spec_im * factor), norm='ortho')
    diff_re = jnp.real(returned) - exit_re
    diff_im = jnp.imag(returned) - exit_im
    object_term = jnp.stack([probe_re * diff_re + probe_im * diff_im, probe_re * diff_im - probe_im * diff_re])
    probe_term = jnp.stack([patch_re * diff_re + patch_im * diff_im, patch_re * diff_im - patch_im * diff_re])
    return (object_term, probe_term)

def reference(object_field, probe_field, measured, positions, counts):
    patch_size = probe_field.shape[1]
    zero_index = jnp.int32(0)

    def visit_slot(loop_state, slot_index):
        accumulator, probe_sum = loop_state
        owner_device = (slot_index // PAT_DEV).astype(jnp.int32)
        is_live = slot_index % PAT_DEV < counts[owner_device]
        top_row = positions[slot_index, 0].astype(jnp.int32)
        left_col = positions[slot_index, 1].astype(jnp.int32)
        object_patch = lax.dynamic_slice(object_field, (zero_index, top_row, left_col), (2, patch_size, patch_size))
        object_term, probe_term = exit_update(object_patch, probe_field, measured[slot_index])
        object_term = jnp.where(is_live, object_term, jnp.zeros_like(object_term))
        probe_term = jnp.where(is_live, probe_term, jnp.zeros_like(probe_term))
        current = lax.dynamic_slice(accumulator, (zero_index, top_row, left_col), (2, patch_size, patch_size))
        accumulator = lax.dynamic_update_slice(accumulator, current + object_term, (zero_index, top_row, left_col))
        return ((accumulator, probe_sum + probe_term), None)
    start = (jnp.zeros_like(object_field), jnp.zeros_like(probe_field))
    slot_ids = jnp.arange(positions.shape[0], dtype=jnp.int32)
    (accumulator, probe_sum), unused = lax.scan(visit_slot, start, slot_ids)
    live_total = jnp.sum(counts).astype(object_field.dtype)
    new_object = object_field + OBJECT_RATE * accumulator
    new_probe = probe_field + probe_sum / jnp.sqrt(live_total)
    return (new_object, new_probe)
```

```python
import functools
import math

import jax
import jax.numpy as jnp
import numpy as np
from jax import lax
from jax.experimental import pallas as pl
from jax.experimental.pallas import tpu as pltpu
from jax.sharding import PartitionSpec as P

FLOOR_SQUARED = 0.25 * 0.25
OBJECT_RATE = 0.5
PIX = 256
HALF = 128
ROWS = 16
F32 = jnp.float32
BF16 = jnp.bfloat16


def split_table(table):
    high = table.astype(jnp.bfloat16)
    low = (table - high.astype(np.float64)).astype(jnp.bfloat16)
    return high, low


def dft_tables():
    freq = np.arange(HALF)[:, None]
    place = np.arange(HALF)[None, :]
    left, right = [], []
    for inverse in (False, True):
        for odd in (0, 1):
            angle = -2.0 * math.pi * (((2 * freq + odd) * place) % PIX) / PIX
            real, imag = np.cos(angle) / 16.0, np.sin(angle) / 16.0
            whole = np.block([[real, -imag], [imag, real]])
            if inverse:
                whole = whole.T
            high, low = split_table(whole)
            left.append(np.concatenate([high, high, low], axis=1))
            high, low = split_table(whole.T)
            right.append(np.concatenate([high, high, low], axis=0))
    return np.stack(left), np.stack(right)


def permute_kernel(first_ref, second_ref, out_ref):
    lane = lax.broadcasted_iota(jnp.int32, (HALF, HALF), 1)
    first = lane < 64
    even_first = jnp.where(first, 2 * lane, 2 * lane - 127)
    odd_first = jnp.where(first, 2 * lane + 1, 2 * lane - 128)
    for parity in range(2):
        rows = pl.ds(parity, HALF, stride=2)
        left = jnp.take_along_axis(first_ref[0, rows, :], even_first, axis=1)
        right = jnp.take_along_axis(second_ref[0, rows, :], odd_first, axis=1)
        out_ref[0, parity * HALF : (parity + 1) * HALF, :HALF] = jnp.where(first, left, right)
        out_ref[0, parity * HALF : (parity + 1) * HALF, HALF:] = pltpu.roll(
            jnp.where(first, right, left), 64, 1
        )


def permuted(measured):
    slots = measured.shape[0]
    return pl.pallas_call(
        permute_kernel,
        grid=(slots,),
        in_specs=[pl.BlockSpec((1, PIX, HALF), lambda s, t=t: (s, 0, t)) for t in range(2)],
        out_specs=pl.BlockSpec((1, PIX, PIX), lambda s: (s, 0, 0)),
        out_shape=jax.ShapeDtypeStruct(measured.shape, F32),
        cost_estimate=pl.CostEstimate(flops=0, bytes_accessed=2 * measured.size * 4, transcendentals=0),
        name="permute_measured",
    )(measured, measured)


def slot_kernel(
    pairs,
    count_ref, top_ref, left_ref,
    object_ref, right_ref, lower_ref, corner_ref, probe_ref, measured_ref, left_tab, right_tab,
    interior_out, right_out, lower_out, probe_out,
    ext, acc, probe2, pacc, patch, probe_r, stack, lanes, spec_e, spec_o, sems,
):
    copies = [
        pltpu.make_async_copy(object_ref, ext.at[:, 0:512, 0:512], sems.at[0]),
        pltpu.make_async_copy(right_ref, ext.at[:, 0:512, 512:768], sems.at[1]),
        pltpu.make_async_copy(lower_ref, ext.at[:, 512:768, 0:512], sems.at[2]),
        pltpu.make_async_copy(corner_ref, ext.at[:, 512:768, 512:768], sems.at[3]),
    ]
    for copy in copies:
        copy.start()
    acc[...] = jnp.zeros_like(acc)
    pacc[...] = jnp.zeros_like(pacc)
    for plane in range(2):
        for tile in range(2):
            value = probe_ref[plane, :, tile * HALF : (tile + 1) * HALF]
            probe2[plane, tile, 0:PIX, :] = value
            probe2[plane, tile, PIX : 2 * PIX, :] = value
    for copy in copies:
        copy.wait()
    count = count_ref[0]
    lane = lax.broadcasted_iota(jnp.int32, (ROWS, HALF), 1)
    sub = lax.broadcasted_iota(jnp.int32, (ROWS, HALF), 0)

    def split(value):
        high = value.astype(BF16)
        return high, (value - high.astype(F32)).astype(BF16)

    def body(step, carry):
        group = []
        for p in range(pairs):
            index = step * pairs + p
            live = index < count
            index = jnp.minimum(index, 15)
            top, left = top_ref[index], left_ref[index]
            group.append(dict(
                p=p, index=index, live=live,
                m_r=top // PIX, s_r=top % PIX, m_c=left // PIX, s_c=left % PIX,
            ))

        for g in group:
            p, s_r, s_c = g["p"], g["s_r"], g["s_c"]
            swap, turn = s_c // HALF, s_c % HALF
            for i in range(HALF // ROWS):
                pieces = {}
                for half in range(2):
                    base = half * HALF + i * ROWS
                    row_far = sub + base < s_r
                    planes = []
                    for plane in range(2):
                        tiles = []
                        rolled = [
                            pltpu.roll(probe2[plane, (t + swap) % 2, pl.ds(PIX - s_r + base, ROWS), :], turn, 1)
                            for t in range(2)
                        ]
                        for t in range(2):
                            col_far = lane + t * HALF < s_c
                            blocks = [
                                [
                                    ext[
                                        plane,
                                        pl.ds(pl.multiple_of((g["m_r"] + dr) * PIX + base, ROWS), ROWS),
                                        pl.ds(pl.multiple_of((g["m_c"] + dc) * PIX + t * HALF, HALF), HALF),
                                    ]
                                    for dc in range(2)
                                ]
                                for dr in range(2)
                            ]
                            near = jnp.where(col_far, blocks[0][1], blocks[0][0])
                            far = jnp.where(col_far, blocks[1][1], blocks[1][0])
                            window = jnp.where(row_far, far, near)
                            patch[p, plane, base : base + ROWS, t * HALF : (t + 1) * HALF] = window
                            q = jnp.where(lane < turn, rolled[1 - t], rolled[t])
                            probe_r[p, plane, base : base + ROWS, t * HALF : (t + 1) * HALF] = q
                            tiles.append((window, q))
                        planes.append(tiles)
                    for t in range(2):
                        (o_re, q_re), (o_im, q_im) = planes[0][t], planes[1][t]
                        pieces[half, t] = (q_re * o_re - q_im * o_im, q_re * o_im + q_im * o_re)
                for t in range(2):
                    for c in range(2):
                        upper, under = pieces[0, t][c], pieces[1, t][c]
                        for j, value in enumerate((upper + under, upper - under)):
                            high, low = split(value)
                            r = c * HALF + i * ROWS
                            stack[p, j, r : r + ROWS, t * HALF : (t + 1) * HALF] = low
                            stack[p, j, PIX + r : PIX + r + ROWS, t * HALF : (t + 1) * HALF] = high

        def left_product(p, j, table):
            both = stack[p, j]
            value = jnp.concatenate([both, both[PIX:]], axis=0)
            return jnp.dot(left_tab[table], value, preferred_element_type=F32)

        def right_product(p, j, table):
            both = lanes[p, j]
            value = jnp.concatenate([both, both[:, PIX:]], axis=1)
            return jnp.dot(value, right_tab[table], preferred_element_type=F32)

        for g in group:
            p = g["p"]
            spec_e[p] = left_product(p, 0, 0)
            spec_o[p] = left_product(p, 1, 1)
        for g in group:
            p = g["p"]
            for half, source in enumerate((spec_e, spec_o)):
                for i in range(HALF // ROWS):
                    r = half * HALF + i * ROWS
                    for c in range(2):
                        s = c * HALF + i * ROWS
                        first = source[p, s : s + ROWS, :HALF]
                        second = source[p, s : s + ROWS, HALF:]
                        for j, value in enumerate((first + second, first - second)):
                            high, low = split(value)
                            lanes[p, j, r : r + ROWS, c * HALF : (c + 1) * HALF] = low
                            lanes[p, j, r : r + ROWS, PIX + c * HALF : PIX + (c + 1) * HALF] = high
        for g in group:
            p = g["p"]
            spec_e[p] = right_product(p, 0, 0)
            spec_o[p] = right_product(p, 1, 1)
        for g in group:
            p = g["p"]
            for j, source in enumerate((spec_e, spec_o)):
                for i in range(PIX // ROWS):
                    r = i * ROWS
                    re = source[p, r : r + ROWS, :HALF]
                    im = source[p, r : r + ROWS, HALF:]
                    amplitude = measured_ref[g["index"], r : r + ROWS, j * HALF : (j + 1) * HALF]
                    factor = amplitude * lax.rsqrt(jnp.maximum(re * re + im * im, FLOOR_SQUARED))
                    for c, value in enumerate((re * factor, im * factor)):
                        high, low = split(value)
                        lanes[p, j, r : r + ROWS, c * HALF : (c + 1) * HALF] = low
                        lanes[p, j, r : r + ROWS, PIX + c * HALF : PIX + (c + 1) * HALF] = high
        for g in group:
            p = g["p"]
            spec_e[p] = right_product(p, 0, 2)
            spec_o[p] = right_product(p, 1, 3)
        for g in group:
            p = g["p"]
            for j in range(2):
                for i in range(HALF // ROWS):
                    r = j * HALF + i * ROWS
                    for c in range(2):
                        first = spec_e[p, r : r + ROWS, c * HALF : (c + 1) * HALF]
                        second = spec_o[p, r : r + ROWS, c * HALF : (c + 1) * HALF]
                        for t, value in enumerate((first + second, first - second)):
                            high, low = split(value)
                            s = c * HALF + i * ROWS
                            stack[p, j, s : s + ROWS, t * HALF : (t + 1) * HALF] = low
                            stack[p, j, PIX + s : PIX + s + ROWS, t * HALF : (t + 1) * HALF] = high
        for g in group:
            p = g["p"]
            spec_e[p] = left_product(p, 0, 2)
            spec_o[p] = left_product(p, 1, 3)
        for g in group:
            p, s_r, s_c = g["p"], g["s_r"], g["s_c"]
            back = (PIX - s_c) % PIX
            swap, turn = back // HALF, back % HALF
            for i in range(HALF // ROWS):
                for half in range(2):
                    base = half * HALF + i * ROWS
                    row_far = sub + base < s_r
                    probe_terms = []
                    for t in range(2):
                        at = (slice(base, base + ROWS), slice(t * HALF, (t + 1) * HALF))
                        col_far = lane + t * HALF < s_c
                        o_re, o_im = patch[(p, 0) + at], patch[(p, 1) + at]
                        q_re, q_im = probe_r[(p, 0) + at], probe_r[(p, 1) + at]
                        diff = []
                        for c in range(2):
                            s = c * HALF + i * ROWS
                            first = spec_e[p, s : s + ROWS, t * HALF : (t + 1) * HALF]
                            second = spec_o[p, s : s + ROWS, t * HALF : (t + 1) * HALF]
                            diff.append(first + second if half == 0 else first - second)
                        d_re = diff[0] - (q_re * o_re - q_im * o_im)
                        d_im = diff[1] - (q_re * o_im + q_im * o_re)
                        d_re = jnp.where(g["live"], d_re, 0.0)
                        d_im = jnp.where(g["live"], d_im, 0.0)
                        terms = (q_re * d_re + q_im * d_im, q_re * d_im - q_im * d_re)
                        probe_terms.append((o_re * d_re + o_im * d_im, o_re * d_im - o_im * d_re))
                        for plane in range(2):
                            for dr in range(2):
                                for dc in range(2):
                                    mine = (row_far if dr else ~row_far) & (col_far if dc else ~col_far)
                                    spot = (
                                        plane,
                                        pl.ds(pl.multiple_of((g["m_r"] + dr) * PIX + base, ROWS), ROWS),
                                        pl.ds(pl.multiple_of((g["m_c"] + dc) * PIX + t * HALF, HALF), HALF),
                                    )
                                    acc[spot] += jnp.where(mine, terms[plane], 0.0)
                    for plane in range(2):
                        rolled = [pltpu.roll(probe_terms[t][plane], turn, 1) for t in range(2)]
                        for t in range(2):
                            value = jnp.where(lane < turn, rolled[1 - t], rolled[t])
                            spot = (plane, (t + swap) % 2, pl.ds(PIX - s_r + base, ROWS), slice(None))
                            pacc[spot] += value
        return carry

    lax.fori_loop(0, (count + pairs - 1) // pairs, body, jnp.int32(0))
    for plane in range(2):
        for tile in range(2):
            probe_out[plane, :, tile * HALF : (tile + 1) * HALF] = (
                pacc[plane, tile, 0:PIX, :] + pacc[plane, tile, PIX : 2 * PIX, :]
            )
    interior_out[...] = ext[:, 0:512, 0:512] + OBJECT_RATE * acc[:, 0:512, 0:512]
    right_out[...] = acc[:, :, 512:768]
    lower_out[...] = acc[:, 512:768, 0:512]


def process(count, tops, lefts, tile, right, lower, corner, probe, measured):
    left_tab, right_tab = dft_tables()
    pairs = 2
    vmem = pl.BlockSpec(memory_space=pltpu.VMEM)
    smem = pl.BlockSpec(memory_space=pltpu.SMEM)
    anywhere = pl.BlockSpec(memory_space=pl.ANY)
    return pl.pallas_call(
        functools.partial(slot_kernel, pairs),
        in_specs=[smem] * 3 + [anywhere] * 4 + [vmem] * 4,
        out_specs=[vmem] * 4,
        out_shape=[
            jax.ShapeDtypeStruct((2, 512, 512), F32),
            jax.ShapeDtypeStruct((2, 768, 256), F32),
            jax.ShapeDtypeStruct((2, 256, 512), F32),
            jax.ShapeDtypeStruct((2, 256, 256), F32),
        ],
        scratch_shapes=[
            pltpu.VMEM((2, 768, 768), F32),
            pltpu.VMEM((2, 768, 768), F32),
            pltpu.VMEM((2, 2, 512, HALF), F32),
            pltpu.VMEM((2, 2, 512, HALF), F32),
            pltpu.VMEM((pairs, 2, PIX, PIX), F32),
            pltpu.VMEM((pairs, 2, PIX, PIX), F32),
            pltpu.VMEM((pairs, 2, 2 * PIX, PIX), BF16),
            pltpu.VMEM((pairs, 2, PIX, 2 * PIX), BF16),
            pltpu.VMEM((pairs, PIX, PIX), F32),
            pltpu.VMEM((pairs, PIX, PIX), F32),
            pltpu.SemaphoreType.DMA((4,)),
        ],
        compiler_params=pltpu.CompilerParams(vmem_limit_bytes=56 * 1024 * 1024),
        cost_estimate=pl.CostEstimate(flops=13 * 10**9, bytes_accessed=12 * 2**20, transcendentals=2**20),
        name="slots",
    )(count, tops, lefts, tile, right, lower, corner, probe, measured, jnp.asarray(left_tab), jnp.asarray(right_tab))


def passed_along(shard, axis, by):
    peers = lax.axis_size(axis)
    pairs = [(i, i + by) for i in range(peers) if 0 <= i + by < peers]
    return lax.ppermute(shard, axis, pairs)


def per_device(object_field, probe_field, measured, positions, counts):
    row_pos = lax.axis_index("row")
    col_pos = lax.axis_index("col")
    own_device = row_pos * lax.axis_size("col") + col_pos
    lower = passed_along(object_field[:, :PIX, :], "row", -1)
    right = passed_along(object_field[:, :, :PIX], "col", -1)
    corner = passed_along(right[:, :PIX, :], "row", -1)
    ordered = permuted(measured)
    tops = positions[:, 0] - row_pos * 512
    lefts = positions[:, 1] - col_pos * 512
    count = counts[own_device][None]
    interior, right_sum, lower_sum, probe_sum = process(
        count, tops, lefts, object_field, right, lower, corner, probe_field, ordered
    )
    probe_total = probe_reduced(probe_sum)
    corner_back = passed_along(right_sum[:, 512:], "row", 1)
    lower_back = passed_along(lower_sum, "row", 1)
    top_right = right_sum[:, :PIX] + corner_back
    top_back = passed_along(top_right, "col", 1)
    bottom_back = passed_along(right_sum[:, PIX:512], "col", 1)
    new_object = interior
    new_object = new_object.at[:, :PIX, :].add(OBJECT_RATE * lower_back)
    new_object = new_object.at[:, :PIX, :PIX].add(OBJECT_RATE * top_back)
    new_object = new_object.at[:, PIX:, :PIX].add(OBJECT_RATE * bottom_back)
    live_total = jnp.sum(counts).astype(F32)
    new_probe = probe_field + probe_total / jnp.sqrt(live_total)
    return (new_object, new_probe)


def probe_reduced(value):
    shape = value.shape
    core = lax.axis_index("row") % 2
    x_pos = lax.axis_index("row") // 2

    def over_core(v):
        return lax.ppermute(v, "row", [(i, i ^ 1) for i in range(8)])

    def over_x(v, k):
        return lax.ppermute(v, "row", [(i, (i + 2 * k) % 8) for i in range(8)])

    def over_y(v, k):
        return lax.ppermute(v, "col", [(i, (i + 4 * k) % 16) for i in range(16)])

    def over_z(v, k):
        return lax.ppermute(v, "col", [(i, i // 4 * 4 + (i % 4 + k) % 4) for i in range(16)])

    def pick(v, i):
        return lax.dynamic_index_in_dim(v, i, 0, False)

    halves = value.reshape(2, 512, 128)
    mine = pick(halves, core) + over_core(pick(halves, 1 - core))
    quarters = mine.reshape(4, 128, 128)
    part = pick(quarters, x_pos)
    for k in (1, 2, 3):
        part = part + over_x(pick(quarters, (x_pos + k) % 4), k)
    part = (part + over_y(part, 2)) + (over_y(part, 1) + over_y(part, 3))
    part = (part + over_z(part, 2)) + (over_z(part, 1) + over_z(part, 3))
    whole = jnp.zeros((4, 128, 128), F32)
    whole = lax.dynamic_update_index_in_dim(whole, part, x_pos, 0)
    for k in (1, 2, 3):
        whole = lax.dynamic_update_index_in_dim(whole, over_x(part, k), (x_pos - k) % 4, 0)
    half = whole.reshape(512, 128)
    other = over_core(half)
    return jnp.concatenate(
        [jnp.where(core == 0, half, other), jnp.where(core == 0, other, half)], axis=0
    ).reshape(shape)


def solution(mesh):
    placed = (
        P(None, "row", "col"),
        P(),
        P(("row", "col"), None, None),
        P(("row", "col"), None),
        P(),
    )
    return jax.shard_map(
        per_device,
        mesh=mesh,
        in_specs=placed,
        out_specs=(P(None, "row", "col"), P()),
        check_vma=False,
    )
```

```python
import functools
import math

import jax
import jax.numpy as jnp
import numpy as np
from jax import lax
from jax.experimental import pallas as pl
from jax.experimental.pallas import tpu as pltpu
from jax.sharding import PartitionSpec as P

FLOOR_SQUARED = 0.25 * 0.25
OBJECT_RATE = 0.5
PIX = 256
HALF = 128
ROWS = 16
F32 = jnp.float32
BF16 = jnp.bfloat16


TILES = 4


def dft_tables():
    freq = np.arange(HALF)[:, None]
    place = np.arange(HALF)[None, :]
    tables = []
    for odd in (0, 1):
        angle = -2.0 * math.pi * (((2 * freq + odd) * place) % PIX) / PIX
        real, imag = np.cos(angle) / 16.0, np.sin(angle) / 16.0
        whole = np.block([[real, -imag], [imag, real]])
        for matrix in (whole, whole.T):
            high = matrix.astype(jnp.bfloat16)
            tables += [high, (matrix - high.astype(np.float64)).astype(jnp.bfloat16)]
    return np.stack(tables)


def split(value):
    high = value.astype(BF16)
    return high, (value - high.astype(F32)).astype(BF16)


def slot_group(group, lane, window_ref, acc_ref, pacc_ref, probe_ref, measured_ref, table_ref, work):
    patch, probe_r, stack, lanes, spec_e, spec_o = work

    for g in group:
        p, turn = g["p"], g["turn"]
        for i in range(HALF // ROWS):
            pieces = {}
            for half in range(2):
                base = half * HALF + i * ROWS
                planes = []
                for plane in range(2):
                    seen = window_ref[plane, pl.ds(g["tile"], 3), pl.ds(g["top"] + base, ROWS), :]
                    window = (jnp.where(lane < turn, seen[2], seen[0]), seen[1])
                    rolled = [
                        pltpu.roll(probe_ref[plane, base : base + ROWS, t * HALF : (t + 1) * HALF], turn, 1)
                        for t in range(2)
                    ]
                    probe = (
                        jnp.where(lane < turn, rolled[1], rolled[0]),
                        jnp.where(lane < turn, rolled[0], rolled[1]),
                    )
                    for t in range(2):
                        at = (p, plane, slice(base, base + ROWS), slice(t * HALF, (t + 1) * HALF))
                        patch[at] = window[t]
                        probe_r[at] = probe[t]
                    planes.append((window, probe))
                for t in range(2):
                    o_re, q_re = planes[0][0][t], planes[0][1][t]
                    o_im, q_im = planes[1][0][t], planes[1][1][t]
                    pieces[half, t] = (q_re * o_re - q_im * o_im, q_re * o_im + q_im * o_re)
            for t in range(2):
                for c in range(2):
                    upper, under = pieces[0, t][c], pieces[1, t][c]
                    for j, value in enumerate((upper + under, upper - under)):
                        high, low = split(value)
                        r = c * HALF + i * ROWS
                        stack[p, j, r : r + ROWS, t * HALF : (t + 1) * HALF] = low
                        stack[p, j, PIX + r : PIX + r + ROWS, t * HALF : (t + 1) * HALF] = high

    def left_product(p, odd, transposed):
        high = table_ref[4 * odd + 2 * transposed]
        low = table_ref[4 * odd + 2 * transposed + 1]
        both = stack[p, odd]
        return jnp.dot(
            jnp.concatenate([high, high, low], axis=1),
            jnp.concatenate([both, both[PIX:]], axis=0),
            preferred_element_type=F32,
        )

    def right_product(p, odd, transposed):
        high = table_ref[4 * odd + 2 * transposed]
        low = table_ref[4 * odd + 2 * transposed + 1]
        both = lanes[p, odd]
        return jnp.dot(
            jnp.concatenate([both, both[:, PIX:]], axis=1),
            jnp.concatenate([high, high, low], axis=0),
            preferred_element_type=F32,
        )

    for g in group:
        p = g["p"]
        spec_e[p] = left_product(p, 0, 0)
        spec_o[p] = left_product(p, 1, 0)
    for g in group:
        p = g["p"]
        for half, source in enumerate((spec_e, spec_o)):
            for i in range(HALF // ROWS):
                r = half * HALF + i * ROWS
                for c in range(2):
                    s = c * HALF + i * ROWS
                    first = source[p, s : s + ROWS, :HALF]
                    second = source[p, s : s + ROWS, HALF:]
                    for j, value in enumerate((first + second, first - second)):
                        high, low = split(value)
                        lanes[p, j, r : r + ROWS, c * HALF : (c + 1) * HALF] = low
                        lanes[p, j, r : r + ROWS, PIX + c * HALF : PIX + (c + 1) * HALF] = high
    for g in group:
        p = g["p"]
        spec_e[p] = right_product(p, 0, 1)
        spec_o[p] = right_product(p, 1, 1)
    for g in group:
        p = g["p"]
        for j, source in enumerate((spec_e, spec_o)):
            for i in range(PIX // ROWS):
                r = i * ROWS
                re = source[p, r : r + ROWS, :HALF]
                im = source[p, r : r + ROWS, HALF:]
                amplitude = measured_ref[g["index"], r : r + ROWS, j * HALF : (j + 1) * HALF]
                factor = amplitude * lax.rsqrt(jnp.maximum(re * re + im * im, FLOOR_SQUARED))
                for c, value in enumerate((re * factor, im * factor)):
                    high, low = split(value)
                    lanes[p, j, r : r + ROWS, c * HALF : (c + 1) * HALF] = low
                    lanes[p, j, r : r + ROWS, PIX + c * HALF : PIX + (c + 1) * HALF] = high
    for g in group:
        p = g["p"]
        spec_e[p] = right_product(p, 0, 0)
        spec_o[p] = right_product(p, 1, 0)
    for g in group:
        p = g["p"]
        for j in range(2):
            for i in range(HALF // ROWS):
                r = j * HALF + i * ROWS
                for c in range(2):
                    first = spec_e[p, r : r + ROWS, c * HALF : (c + 1) * HALF]
                    second = spec_o[p, r : r + ROWS, c * HALF : (c + 1) * HALF]
                    for t, value in enumerate((first + second, first - second)):
                        high, low = split(value)
                        s = c * HALF + i * ROWS
                        stack[p, j, s : s + ROWS, t * HALF : (t + 1) * HALF] = low
                        stack[p, j, PIX + s : PIX + s + ROWS, t * HALF : (t + 1) * HALF] = high
    for g in group:
        p = g["p"]
        spec_e[p] = left_product(p, 0, 1)
        spec_o[p] = left_product(p, 1, 1)
    for g in group:
        p, turn = g["p"], g["turn"]
        back = (HALF - turn) % HALF
        for i in range(HALF // ROWS):
            for half in range(2):
                base = half * HALF + i * ROWS
                rows = slice(base, base + ROWS)
                object_terms, probe_terms = [], []
                for t in range(2):
                    cols = slice(t * HALF, (t + 1) * HALF)
                    o_re, o_im = patch[p, 0, rows, cols], patch[p, 1, rows, cols]
                    q_re, q_im = probe_r[p, 0, rows, cols], probe_r[p, 1, rows, cols]
                    found = []
                    for c in range(2):
                        s = c * HALF + i * ROWS
                        first = spec_e[p, s : s + ROWS, cols]
                        second = spec_o[p, s : s + ROWS, cols]
                        found.append(first + second if half == 0 else first - second)
                    d_re = jnp.where(g["live"], found[0] - (q_re * o_re - q_im * o_im), 0.0)
                    d_im = jnp.where(g["live"], found[1] - (q_re * o_im + q_im * o_re), 0.0)
                    object_terms.append((q_re * d_re + q_im * d_im, q_re * d_im - q_im * d_re))
                    probe_terms.append((o_re * d_re + o_im * d_im, o_re * d_im - o_im * d_re))
                spots = [
                    (plane, pl.ds(g["tile"], 3), pl.ds(g["top"] + base, ROWS), slice(None)) for plane in range(2)
                ]
                held = [acc_ref[spot] for spot in spots]
                for plane in range(2):
                    mixed, pure = object_terms[0][plane], object_terms[1][plane]
                    acc_ref[spots[plane]] = jnp.stack([
                        held[plane][0] + jnp.where(lane < turn, 0.0, mixed),
                        held[plane][1] + pure,
                        held[plane][2] + jnp.where(lane < turn, mixed, 0.0),
                    ])
                for plane in range(2):
                    rolled = [pltpu.roll(probe_terms[t][plane], back, 1) for t in range(2)]
                    part = slice(i * ROWS, (i + 1) * ROWS)
                    pacc_ref[plane, half, part, :] += jnp.where(lane < HALF - turn, rolled[0], rolled[1])
                    pacc_ref[plane, 2 + half, part, :] += jnp.where(lane < HALF - turn, rolled[1], rolled[0])


def slot_loop(pairs, local, count_ref, top_ref, left_ref, order, refs):
    lane = lax.broadcasted_iota(jnp.int32, (ROWS, HALF), 1)

    def enlist(s, n):
        inside = (top_ref[s] <= PIX) & (left_ref[s] <= PIX)
        mine = inside if local else jnp.logical_not(inside)

        @pl.when(mine)
        def _():
            order[n] = s

        return n + mine.astype(jnp.int32)

    total = lax.fori_loop(jnp.int32(0), count_ref[0], enlist, jnp.int32(0))

    def body(step, carry):
        group = []
        for p in range(pairs):
            place = step * pairs + p
            index = order[jnp.minimum(place, total - 1)]
            left = left_ref[index]
            group.append(dict(
                p=p, index=index, live=place < total, top=top_ref[index], tile=left // HALF, turn=left % HALF,
            ))
        slot_group(group, lane, *refs)
        return carry

    lax.fori_loop(jnp.int32(0), (total + pairs - 1) // pairs, body, jnp.int32(0))


def order_kernel(count_ref, measured_ref, ordered_out, raw, sems):
    copies = [
        pltpu.make_async_copy(measured_ref.at[:, :, pl.ds(t * HALF, HALF)], raw.at[t], sems.at[t])
        for t in range(2)
    ]
    for copy in copies:
        copy.start()
    lane = lax.broadcasted_iota(jnp.int32, (HALF, HALF), 1)
    first = lane < 64
    even_first = jnp.where(first, 2 * lane, 2 * lane - 127)
    odd_first = jnp.where(first, 2 * lane + 1, 2 * lane - 128)
    for copy in copies:
        copy.wait()

    def reorder(s, carry):
        for parity in range(2):
            rows = pl.ds(parity, HALF, stride=2)
            left = jnp.take_along_axis(raw[0, s, rows, :], even_first, axis=1)
            right = jnp.take_along_axis(raw[1, s, rows, :], odd_first, axis=1)
            out = slice(parity * HALF, (parity + 1) * HALF)
            ordered_out[s, out, :HALF] = jnp.where(first, left, right)
            ordered_out[s, out, HALF:] = pltpu.roll(jnp.where(first, right, left), 64, 1)
        return carry

    lax.fori_loop(jnp.int32(0), count_ref[0], reorder, jnp.int32(0))


def local_kernel(
    pairs,
    count_ref, top_ref, left_ref, object_ref, ordered_ref, probe_ref, table_ref,
    acc_out, pacc_out,
    ext, order, sems, *work,
):
    copies = [
        pltpu.make_async_copy(object_ref.at[:, :, pl.ds(t * HALF, HALF)], ext.at[:, t], sems.at[t])
        for t in range(TILES)
    ]
    for copy in copies:
        copy.start()
    acc_out[...] = jnp.zeros_like(acc_out)
    pacc_out[...] = jnp.zeros_like(pacc_out)
    for copy in copies:
        copy.wait()
    slot_loop(
        pairs, True, count_ref, top_ref, left_ref, order,
        (ext, acc_out, pacc_out, probe_ref, ordered_ref, table_ref, work),
    )


def rest_kernel(
    pairs,
    count_ref, top_ref, left_ref, place_ref, object_ref, top_rim, bottom_rim, lower_rim, corner_rim, held_ref,
    pacc_ref, ordered_ref, probe_ref, table_ref,
    tile_out, top_out, bottom_out, lower_out, mine_out, other_out,
    ext, acc, pacc, order, sems, *work,
):
    copies = []

    def bring(source, target):
        copies.append(pltpu.make_async_copy(source, target, sems.at[len(copies)]))
        copies[-1].start()

    for t in range(TILES):
        cols = pl.ds(t * HALF, HALF)
        bring(object_ref.at[:, :, cols], ext.at[:, t, pl.ds(0, 512)])
        bring(lower_rim.at[:, :, cols], ext.at[:, t, pl.ds(512, PIX)])
        bring(held_ref.at[:, t], acc.at[:, t, pl.ds(0, 512)])
    for t in range(2):
        cols = pl.ds(t * HALF, HALF)
        bring(top_rim.at[:, :, cols], ext.at[:, TILES + t, pl.ds(0, PIX)])
        bring(bottom_rim.at[:, :, cols], ext.at[:, TILES + t, pl.ds(PIX, PIX)])
        bring(corner_rim.at[:, :, cols], ext.at[:, TILES + t, pl.ds(512, PIX)])
    acc[:, 0:TILES, 512:768, :] = jnp.zeros((2, TILES, PIX, HALF), F32)
    acc[:, TILES:, :, :] = jnp.zeros((2, 2, 768, HALF), F32)
    pacc[...] = pacc_ref[...]
    for copy in copies:
        copy.wait()
    slot_loop(
        pairs, False, count_ref, top_ref, left_ref, order,
        (ext, acc, pacc, probe_ref, ordered_ref, table_ref, work),
    )
    y_pos, core = place_ref[0], place_ref[1]
    for k in range(4):
        mine_out[k] = pacc[core, (y_pos + k) % 4]
        other_out[k] = pacc[1 - core, (y_pos + k) % 4]
    for t in range(TILES):
        cols = slice(t * HALF, (t + 1) * HALF)
        tile_out[:, :, cols] = ext[:, t, 0:512, :] + OBJECT_RATE * acc[:, t, 0:512, :]
    for t in range(TILES + 2):
        lower_out[:, :, t * HALF : (t + 1) * HALF] = OBJECT_RATE * acc[:, t, 512:768, :]
    for t in range(2):
        cols = slice(t * HALF, (t + 1) * HALF)
        top_out[:, :, cols] = OBJECT_RATE * acc[:, TILES + t, 0:PIX, :]
        bottom_out[:, :, cols] = OBJECT_RATE * acc[:, TILES + t, PIX:512, :]


VMEM = pl.BlockSpec(memory_space=pltpu.VMEM)
SMEM = pl.BlockSpec(memory_space=pltpu.SMEM)
ANYWHERE = pl.BlockSpec(memory_space=pl.ANY)


def work_shapes(pairs):
    return [
        pltpu.VMEM((pairs, 2, PIX, PIX), F32),
        pltpu.VMEM((pairs, 2, PIX, PIX), F32),
        pltpu.VMEM((pairs, 2, 2 * PIX, PIX), BF16),
        pltpu.VMEM((pairs, 2, PIX, 2 * PIX), BF16),
        pltpu.VMEM((pairs, PIX, PIX), F32),
        pltpu.VMEM((pairs, PIX, PIX), F32),
    ]


QUARTER = jax.ShapeDtypeStruct((HALF, HALF), F32)
QUARTERS = jax.ShapeDtypeStruct((4, HALF, HALF), F32)
WHOLE_TILE = jax.ShapeDtypeStruct((2, 512, 512), F32)
LOWER = jax.ShapeDtypeStruct((2, PIX, 768), F32)
TOKEN = jax.ShapeDtypeStruct((8, HALF), F32)
BLOCK = jax.ShapeDtypeStruct((2, PIX, PIX), F32)


def in_order(count, measured):
    return pl.pallas_call(
        order_kernel,
        in_specs=[SMEM, ANYWHERE],
        out_specs=VMEM,
        out_shape=jax.ShapeDtypeStruct((16, PIX, PIX), F32),
        scratch_shapes=[pltpu.VMEM((2, 16, PIX, HALF), F32), pltpu.SemaphoreType.DMA((2,))],
        compiler_params=pltpu.CompilerParams(vmem_limit_bytes=10 * 1024 * 1024),
        cost_estimate=pl.CostEstimate(flops=0, bytes_accessed=16 * 2**20, transcendentals=0),
        name="order_measured",
    )(count, measured)


def process_local(count, tops, lefts, tile, ordered, probe, tables):
    pairs = 2
    return pl.pallas_call(
        functools.partial(local_kernel, pairs),
        in_specs=[SMEM] * 3 + [ANYWHERE] + [VMEM] * 3,
        out_specs=[VMEM] * 2,
        out_shape=[jax.ShapeDtypeStruct((2, TILES + 1, 512, HALF), F32), jax.ShapeDtypeStruct((2, 4, HALF, HALF), F32)],
        scratch_shapes=[
            pltpu.VMEM((2, TILES + 1, 512, HALF), F32),
            pltpu.SMEM((16,), jnp.int32),
            pltpu.SemaphoreType.DMA((TILES,)),
        ] + work_shapes(pairs),
        compiler_params=pltpu.CompilerParams(vmem_limit_bytes=22 * 1024 * 1024),
        cost_estimate=pl.CostEstimate(flops=6 * 10**9, bytes_accessed=20 * 2**20, transcendentals=2**20),
        name="local_slots",
    )(count, tops, lefts, tile, ordered, probe, tables)


def process_rest(count, tops, lefts, place, tile, top, bottom, lower, corner, held, pacc, ordered, probe, tables):
    pairs = 2
    return pl.pallas_call(
        functools.partial(rest_kernel, pairs),
        in_specs=[SMEM] * 4 + [ANYWHERE] * 6 + [VMEM] * 4,
        out_specs=[VMEM] * 6,
        out_shape=[WHOLE_TILE] + [BLOCK] * 2 + [LOWER] + [QUARTERS] * 2,
        scratch_shapes=[
            pltpu.VMEM((2, TILES + 2, 768, HALF), F32),
            pltpu.VMEM((2, TILES + 2, 768, HALF), F32),
            pltpu.VMEM((2, 4, HALF, HALF), F32),
            pltpu.SMEM((16,), jnp.int32),
            pltpu.SemaphoreType.DMA((18,)),
        ] + work_shapes(pairs),
        compiler_params=pltpu.CompilerParams(vmem_limit_bytes=30 * 1024 * 1024),
        cost_estimate=pl.CostEstimate(flops=13 * 10**9, bytes_accessed=20 * 2**20, transcendentals=2**20),
        name="other_slots",
    )(count, tops, lefts, place, tile, top, bottom, lower, corner, held, pacc, ordered, probe, tables)


def joined(kernel, name, operands, outs, smem=0, beside=()):
    return pl.pallas_call(
        kernel,
        in_specs=[SMEM] * smem + [VMEM] * (len(operands) - smem) + [ANYWHERE] * len(beside),
        out_specs=[VMEM] * len(outs),
        out_shape=list(outs),
        compiler_params=pltpu.CompilerParams(vmem_limit_bytes=16 * 1024 * 1024),
        cost_estimate=pl.CostEstimate(flops=2**18, bytes_accessed=2**20, transcendentals=0),
        name=name,
    )(*operands, *beside)


def pair_kernel(mine_ref, came_ref, *outs):
    for k, out in enumerate(outs):
        out[...] = mine_ref[k] + came_ref[k]


def ring_kernel(own, one, two, three, *rest):
    rest[-1][...] = (own[...] + two[...]) + (one[...] + three[...])


def corner_kernel(own, one, two, three, top, lower, bottom, part, rim):
    ring_kernel(own, one, two, three, part)
    rim[...] = top[...] + lower[:, :, 512:]


def tile_kernel(tile, top, bottom, lower, out, token):
    out[:, :PIX, :PIX] = tile[:, :PIX, :PIX] + (lower[:, :, :PIX] + top[...])
    out[:, :PIX, PIX:] = tile[:, :PIX, PIX:] + lower[:, :, PIX:512]
    out[:, PIX:, :PIX] = tile[:, PIX:, :PIX] + bottom[...]
    out[:, PIX:, PIX:] = tile[:, PIX:, PIX:]
    token[...] = jnp.zeros_like(token)


def half_kernel(place_ref, own, one, two, three, token, half):
    for k, part in enumerate((own, one, two, three)):
        half[(place_ref[0] + 4 - k) % 4] = part[...]


def probe_kernel(place_ref, root_ref, probe, half, other, out):
    core, root = place_ref[1], root_ref[0]
    for q in range(4):
        at = (slice(q % 2 * HALF, (q % 2 + 1) * HALF), slice(q // 2 * HALF, (q // 2 + 1) * HALF))
        mine, theirs = half[q], other[q]
        out[(0,) + at] = probe[(0,) + at] + jnp.where(core == 0, mine, theirs) / root
        out[(1,) + at] = probe[(1,) + at] + jnp.where(core == 0, theirs, mine) / root


def passed_along(shard, axis, by):
    peers = lax.axis_size(axis)
    pairs = [(i, i + by) for i in range(peers) if 0 <= i + by < peers]
    return lax.ppermute(shard, axis, pairs)


def over_core(v):
    return lax.ppermute(v, "row", [(i, i ^ 1) for i in range(8)])


def over_x(v, k):
    return lax.ppermute(v, "row", [(i, (i + 2 * k) % 8) for i in range(8)])


def over_y(v, k):
    return lax.ppermute(v, "col", [(i, (i + 4 * k) % 16) for i in range(16)])


def over_z(v, k):
    return lax.ppermute(v, "col", [(i, i // 4 * 4 + (i % 4 + k) % 4) for i in range(16)])


def per_device(object_field, probe_field, measured, positions, counts):
    row_pos = lax.axis_index("row")
    col_pos = lax.axis_index("col")
    own_device = row_pos * lax.axis_size("col") + col_pos
    place = jnp.stack([col_pos // 4, row_pos % 2])
    root = jnp.sqrt(jnp.sum(counts).astype(F32))[None]
    tables = jnp.asarray(dft_tables())
    top = passed_along(object_field[:, :PIX, :PIX], "col", -1)
    bottom = passed_along(object_field[:, PIX:, :PIX], "col", -1)
    lower = passed_along(object_field[:, :PIX, :], "row", -1)
    corner = passed_along(top, "row", -1)
    count = counts[own_device][None]
    where = (count, positions[:, 0] - row_pos * 512, positions[:, 1] - col_pos * 512)
    ordered = in_order(count, measured)
    held, pacc = process_local(*where, object_field, ordered, probe_field, tables)
    tile, top_sum, bottom_sum, lower_sum, mine, other = process_rest(
        *where, place, object_field, top, bottom, lower, corner, held, pacc, ordered, probe_field, tables
    )
    lower_back = passed_along(lower_sum, "row", 1)
    bottom_back = passed_along(bottom_sum, "col", 1)
    quarters = joined(pair_kernel, "pair_sum", (mine, over_core(other)), [QUARTER] * 4)
    (part,) = joined(
        ring_kernel, "y_sum", [quarters[0]] + [over_y(quarters[k], k) for k in (1, 2, 3)], [QUARTER], beside=[root]
    )
    part, rim = joined(
        corner_kernel, "z_sum", [part] + [over_z(part, k) for k in (1, 2, 3)] + [top_sum, lower_back],
        [QUARTER, BLOCK], beside=[bottom_back],
    )
    top_back = passed_along(rim, "col", 1)
    (part,) = joined(ring_kernel, "x_sum", [part] + [over_x(part, k) for k in (1, 2, 3)], [QUARTER])
    new_object, token = joined(
        tile_kernel, "new_tile", (tile, top_back, bottom_back, lower_back), [WHOLE_TILE, TOKEN]
    )
    (half,) = joined(
        half_kernel, "half", [place, part] + [over_y(part, k) for k in (1, 2, 3)], [QUARTERS], smem=1,
        beside=[token],
    )
    (new_probe,) = joined(
        probe_kernel, "new_probe", (place, root, probe_field, half, over_core(half)), [BLOCK], smem=2,
    )
    return (new_object, new_probe)


def solution(mesh):
    placed = (
        P(None, "row", "col"),
        P(),
        P(("row", "col"), None, None),
        P(("row", "col"), None),
        P(),
    )
    return jax.shard_map(
        per_device,
        mesh=mesh,
        in_specs=placed,
        out_specs=(P(None, "row", "col"), P()),
        check_vma=False,
    )
```

```python
import functools
import math

import jax
import jax.numpy as jnp
import numpy as np
from jax import lax
from jax.experimental import pallas as pl
from jax.experimental.pallas import tpu as pltpu
from jax.sharding import PartitionSpec as P

FLOOR_SQUARED = 0.25 * 0.25
OBJECT_RATE = 0.5
PIX = 256
HALF = 128
ROWS = 16
F32 = jnp.float32
BF16 = jnp.bfloat16


TILES = 4


def dft_tables():
    freq = np.arange(HALF)[:, None]
    place = np.arange(HALF)[None, :]
    tables = []
    for odd in (0, 1):
        angle = -2.0 * math.pi * (((2 * freq + odd) * place) % PIX) / PIX
        real, imag = np.cos(angle) / 16.0, np.sin(angle) / 16.0
        whole = np.block([[real, -imag], [imag, real]])
        for matrix in (whole, whole.T):
            high = matrix.astype(jnp.bfloat16)
            tables += [high, (matrix - high.astype(np.float64)).astype(jnp.bfloat16)]
    return np.stack(tables)


def split(value):
    high = value.astype(BF16)
    return high, (value - high.astype(F32)).astype(BF16)


def slot_group(group, lane, window_ref, acc_ref, pacc_ref, probe_ref, measured_ref, table_ref, work):
    patch, probe_r, stack, lanes, spec_e, spec_o = work

    for g in group:
        p, turn = g["p"], g["turn"]
        for i in range(HALF // ROWS):
            pieces = {}
            for half in range(2):
                base = half * HALF + i * ROWS
                planes = []
                for plane in range(2):
                    seen = window_ref[plane, pl.ds(g["tile"], 3), pl.ds(g["top"] + base, ROWS), :]
                    window = (jnp.where(lane < turn, seen[2], seen[0]), seen[1])
                    rolled = [
                        pltpu.roll(probe_ref[plane, base : base + ROWS, t * HALF : (t + 1) * HALF], turn, 1)
                        for t in range(2)
                    ]
                    probe = (
                        jnp.where(lane < turn, rolled[1], rolled[0]),
                        jnp.where(lane < turn, rolled[0], rolled[1]),
                    )
                    for t in range(2):
                        at = (p, plane, slice(base, base + ROWS), slice(t * HALF, (t + 1) * HALF))
                        patch[at] = window[t]
                        probe_r[at] = probe[t]
                    planes.append((window, probe))
                for t in range(2):
                    o_re, q_re = planes[0][0][t], planes[0][1][t]
                    o_im, q_im = planes[1][0][t], planes[1][1][t]
                    pieces[half, t] = (q_re * o_re - q_im * o_im, q_re * o_im + q_im * o_re)
            for t in range(2):
                for c in range(2):
                    upper, under = pieces[0, t][c], pieces[1, t][c]
                    for j, value in enumerate((upper + under, upper - under)):
                        high, low = split(value)
                        r = c * HALF + i * ROWS
                        stack[p, j, r : r + ROWS, t * HALF : (t + 1) * HALF] = low
                        stack[p, j, PIX + r : PIX + r + ROWS, t * HALF : (t + 1) * HALF] = high

    def left_product(p, odd, transposed):
        high = table_ref[4 * odd + 2 * transposed]
        low = table_ref[4 * odd + 2 * transposed + 1]
        both = stack[p, odd]
        return jnp.dot(
            jnp.concatenate([high, high, low], axis=1),
            jnp.concatenate([both, both[PIX:]], axis=0),
            preferred_element_type=F32,
        )

    def right_product(p, odd, transposed):
        high = table_ref[4 * odd + 2 * transposed]
        low = table_ref[4 * odd + 2 * transposed + 1]
        both = lanes[p, odd]
        return jnp.dot(
            jnp.concatenate([both, both[:, PIX:]], axis=1),
            jnp.concatenate([high, high, low], axis=0),
            preferred_element_type=F32,
        )

    for g in group:
        p = g["p"]
        spec_e[p] = left_product(p, 0, 0)
        spec_o[p] = left_product(p, 1, 0)
    for g in group:
        p = g["p"]
        for half, source in enumerate((spec_e, spec_o)):
            for i in range(HALF // ROWS):
                r = half * HALF + i * ROWS
                for c in range(2):
                    s = c * HALF + i * ROWS
                    first = source[p, s : s + ROWS, :HALF]
                    second = source[p, s : s + ROWS, HALF:]
                    for j, value in enumerate((first + second, first - second)):
                        high, low = split(value)
                        lanes[p, j, r : r + ROWS, c * HALF : (c + 1) * HALF] = low
                        lanes[p, j, r : r + ROWS, PIX + c * HALF : PIX + (c + 1) * HALF] = high
    for g in group:
        p = g["p"]
        spec_e[p] = right_product(p, 0, 1)
        spec_o[p] = right_product(p, 1, 1)
    for g in group:
        p = g["p"]
        for j, source in enumerate((spec_e, spec_o)):
            for i in range(PIX // ROWS):
                r = i * ROWS
                re = source[p, r : r + ROWS, :HALF]
                im = source[p, r : r + ROWS, HALF:]
                amplitude = measured_ref[g["index"], r : r + ROWS, j * HALF : (j + 1) * HALF]
                factor = amplitude * lax.rsqrt(jnp.maximum(re * re + im * im, FLOOR_SQUARED))
                for c, value in enumerate((re * factor, im * factor)):
                    high, low = split(value)
                    lanes[p, j, r : r + ROWS, c * HALF : (c + 1) * HALF] = low
                    lanes[p, j, r : r + ROWS, PIX + c * HALF : PIX + (c + 1) * HALF] = high
    for g in group:
        p = g["p"]
        spec_e[p] = right_product(p, 0, 0)
        spec_o[p] = right_product(p, 1, 0)
    for g in group:
        p = g["p"]
        for j in range(2):
            for i in range(HALF // ROWS):
                r = j * HALF + i * ROWS
                for c in range(2):
                    first = spec_e[p, r : r + ROWS, c * HALF : (c + 1) * HALF]
                    second = spec_o[p, r : r + ROWS, c * HALF : (c + 1) * HALF]
                    for t, value in enumerate((first + second, first - second)):
                        high, low = split(value)
                        s = c * HALF + i * ROWS
                        stack[p, j, s : s + ROWS, t * HALF : (t + 1) * HALF] = low
                        stack[p, j, PIX + s : PIX + s + ROWS, t * HALF : (t + 1) * HALF] = high
    for g in group:
        p = g["p"]
        spec_e[p] = left_product(p, 0, 1)
        spec_o[p] = left_product(p, 1, 1)
    for g in group:
        p, turn = g["p"], g["turn"]
        back = (HALF - turn) % HALF
        for i in range(HALF // ROWS):
            for half in range(2):
                base = half * HALF + i * ROWS
                rows = slice(base, base + ROWS)
                object_terms, probe_terms = [], []
                for t in range(2):
                    cols = slice(t * HALF, (t + 1) * HALF)
                    o_re, o_im = patch[p, 0, rows, cols], patch[p, 1, rows, cols]
                    q_re, q_im = probe_r[p, 0, rows, cols], probe_r[p, 1, rows, cols]
                    found = []
                    for c in range(2):
                        s = c * HALF + i * ROWS
                        first = spec_e[p, s : s + ROWS, cols]
                        second = spec_o[p, s : s + ROWS, cols]
                        found.append(first + second if half == 0 else first - second)
                    d_re = jnp.where(g["live"], found[0] - (q_re * o_re - q_im * o_im), 0.0)
                    d_im = jnp.where(g["live"], found[1] - (q_re * o_im + q_im * o_re), 0.0)
                    object_terms.append((q_re * d_re + q_im * d_im, q_re * d_im - q_im * d_re))
                    probe_terms.append((o_re * d_re + o_im * d_im, o_re * d_im - o_im * d_re))
                spots = [
                    (plane, pl.ds(g["tile"], 3), pl.ds(g["top"] + base, ROWS), slice(None)) for plane in range(2)
                ]
                held = [acc_ref[spot] for spot in spots]
                for plane in range(2):
                    mixed, pure = object_terms[0][plane], object_terms[1][plane]
                    acc_ref[spots[plane]] = jnp.stack([
                        held[plane][0] + jnp.where(lane < turn, 0.0, mixed),
                        held[plane][1] + pure,
                        held[plane][2] + jnp.where(lane < turn, mixed, 0.0),
                    ])
                for plane in range(2):
                    rolled = [pltpu.roll(probe_terms[t][plane], back, 1) for t in range(2)]
                    part = slice(i * ROWS, (i + 1) * ROWS)
                    pacc_ref[plane, half, part, :] += jnp.where(lane < HALF - turn, rolled[0], rolled[1])
                    pacc_ref[plane, 2 + half, part, :] += jnp.where(lane < HALF - turn, rolled[1], rolled[0])


EARLY = 4


def own_count(counts_ref):
    return counts_ref[lax.axis_index("row") * lax.axis_size("col") + lax.axis_index("col")]


def slot_loop(pairs, stage, counts_ref, positions_ref, order, refs):
    lane = lax.broadcasted_iota(jnp.int32, (ROWS, HALF), 1)
    above, before = lax.axis_index("row") * 512, lax.axis_index("col") * 512

    def enlist(s, carry):
        n, early = carry
        beside = positions_ref[1, s] - before <= PIX
        first = beside & (positions_ref[0, s] - above <= PIX) & (early < EARLY)
        if stage == 0:
            mine = first
        elif stage == 1:
            mine = beside & jnp.logical_not(first)
        else:
            mine = jnp.logical_not(beside)

        @pl.when(mine)
        def _():
            order[n] = s

        return n + mine.astype(jnp.int32), early + first.astype(jnp.int32)

    total, _ = lax.fori_loop(jnp.int32(0), own_count(counts_ref), enlist, (jnp.int32(0), jnp.int32(0)))

    def body(step, carry):
        group = []
        for p in range(pairs):
            place = step * pairs + p
            index = order[jnp.minimum(place, total - 1)]
            top, left = positions_ref[0, index] - above, positions_ref[1, index] - before
            group.append(dict(
                p=p, index=index, live=place < total, top=top, tile=left // HALF, turn=left % HALF,
            ))
        slot_group(group, lane, *refs)
        return carry

    lax.fori_loop(jnp.int32(0), (total + pairs - 1) // pairs, body, jnp.int32(0))


def early_kernel(
    pairs,
    counts_ref, positions_ref, measured_ref, object_ref, probe_ref, table_ref,
    ordered_out, acc_out, pacc_out,
    raw, ext, order, sems, tile_sems, *work,
):
    tiles = [
        pltpu.make_async_copy(object_ref.at[:, :, pl.ds(t * HALF, HALF)], ext.at[:, t], tile_sems.at[t])
        for t in range(TILES)
    ]

    def coming(s, t):
        return pltpu.make_async_copy(measured_ref.at[s, :, pl.ds(t * HALF, HALF)], raw.at[s, t], sems.at[s, t])

    for s in range(16):
        for t in range(2):
            coming(s, t).start()
    for copy in tiles:
        copy.start()
    acc_out[...] = jnp.zeros_like(acc_out)
    pacc_out[...] = jnp.zeros_like(pacc_out)
    lane = lax.broadcasted_iota(jnp.int32, (HALF, HALF), 1)
    first = lane < 64
    even_first = jnp.where(first, 2 * lane, 2 * lane - 127)
    odd_first = jnp.where(first, 2 * lane + 1, 2 * lane - 128)

    def reorder(s, carry):
        for t in range(2):
            coming(s, t).wait()
        for parity in range(2):
            rows = pl.ds(parity, HALF, stride=2)
            left = jnp.take_along_axis(raw[s, 0, rows, :], even_first, axis=1)
            right = jnp.take_along_axis(raw[s, 1, rows, :], odd_first, axis=1)
            out = slice(parity * HALF, (parity + 1) * HALF)
            ordered_out[s, out, :HALF] = jnp.where(first, left, right)
            ordered_out[s, out, HALF:] = pltpu.roll(jnp.where(first, right, left), 64, 1)
        return carry

    def skip(s, carry):
        for t in range(2):
            coming(s, t).wait()
        return carry

    count = own_count(counts_ref)
    lax.fori_loop(jnp.int32(0), count, reorder, jnp.int32(0))
    lax.fori_loop(count, jnp.int32(16), skip, jnp.int32(0))
    for copy in tiles:
        copy.wait()
    slot_loop(
        pairs, 0, counts_ref, positions_ref, order,
        (ext, acc_out, pacc_out, probe_ref, ordered_out, table_ref, work),
    )


def local_kernel(
    pairs,
    counts_ref, positions_ref, object_ref, lower_rim, held_ref, pacc_ref, ordered_ref, probe_ref, table_ref,
    acc_out, pacc_out,
    ext, order, sems, *work,
):
    copies = []
    for t in range(TILES):
        cols = pl.ds(t * HALF, HALF)
        copies.append(pltpu.make_async_copy(object_ref.at[:, :, cols], ext.at[:, t, pl.ds(0, 512)], sems.at[2 * t]))
        copies.append(
            pltpu.make_async_copy(lower_rim.at[:, :, cols], ext.at[:, t, pl.ds(512, PIX)], sems.at[2 * t + 1])
        )
    for copy in copies:
        copy.start()
    acc_out[:, :, 0:512, :] = held_ref[...]
    acc_out[:, :, 512:768, :] = jnp.zeros((2, TILES + 1, PIX, HALF), F32)
    pacc_out[...] = pacc_ref[...]
    for copy in copies:
        copy.wait()
    slot_loop(
        pairs, 1, counts_ref, positions_ref, order,
        (ext, acc_out, pacc_out, probe_ref, ordered_ref, table_ref, work),
    )


def rest_kernel(
    pairs,
    counts_ref, positions_ref, object_ref, top_rim, bottom_rim, lower_rim, corner_rim, held_ref,
    pacc_ref, ordered_ref, probe_ref, table_ref,
    tile_out, top_out, bottom_out, lower_out, mine_out, other_out,
    ext, acc, pacc, order, sems, *work,
):
    copies = []

    def bring(source, target):
        copies.append(pltpu.make_async_copy(source, target, sems.at[len(copies)]))
        copies[-1].start()

    for t in range(TILES):
        cols = pl.ds(t * HALF, HALF)
        bring(object_ref.at[:, :, cols], ext.at[:, t, pl.ds(0, 512)])
        bring(lower_rim.at[:, :, cols], ext.at[:, t, pl.ds(512, PIX)])
        bring(held_ref.at[:, t], acc.at[:, t])
    for t in range(2):
        cols = pl.ds(t * HALF, HALF)
        bring(top_rim.at[:, :, cols], ext.at[:, TILES + t, pl.ds(0, PIX)])
        bring(bottom_rim.at[:, :, cols], ext.at[:, TILES + t, pl.ds(PIX, PIX)])
        bring(corner_rim.at[:, :, cols], ext.at[:, TILES + t, pl.ds(512, PIX)])
    acc[:, TILES:, :, :] = jnp.zeros((2, 2, 768, HALF), F32)
    pacc[...] = pacc_ref[...]
    for copy in copies:
        copy.wait()
    slot_loop(
        pairs, 2, counts_ref, positions_ref, order,
        (ext, acc, pacc, probe_ref, ordered_ref, table_ref, work),
    )
    y_pos, core = lax.axis_index("col") // 4, lax.axis_index("row") % 2
    for k in range(4):
        mine_out[k] = pacc[core, (y_pos + k) % 4]
        other_out[k] = pacc[1 - core, (y_pos + k) % 4]
    leaving = []
    for t in range(TILES):
        ext[:, t, 0:512, :] = ext[:, t, 0:512, :] + OBJECT_RATE * acc[:, t, 0:512, :]
        leaving.append(
            pltpu.make_async_copy(ext.at[:, t, pl.ds(0, 512)], tile_out.at[:, :, pl.ds(t * HALF, HALF)], sems.at[t])
        )
        leaving[-1].start()
    for t in range(TILES + 2):
        lower_out[:, :, t * HALF : (t + 1) * HALF] = OBJECT_RATE * acc[:, t, 512:768, :]
    for t in range(2):
        cols = slice(t * HALF, (t + 1) * HALF)
        top_out[:, :, cols] = OBJECT_RATE * acc[:, TILES + t, 0:PIX, :]
        bottom_out[:, :, cols] = OBJECT_RATE * acc[:, TILES + t, PIX:512, :]
    for copy in leaving:
        copy.wait()


VMEM = pl.BlockSpec(memory_space=pltpu.VMEM)
SMEM = pl.BlockSpec(memory_space=pltpu.SMEM)
ANYWHERE = pl.BlockSpec(memory_space=pl.ANY)
HBM = pl.BlockSpec(memory_space=pltpu.HBM)


def work_shapes(pairs):
    return [
        pltpu.VMEM((pairs, 2, PIX, PIX), F32),
        pltpu.VMEM((pairs, 2, PIX, PIX), F32),
        pltpu.VMEM((pairs, 2, 2 * PIX, PIX), BF16),
        pltpu.VMEM((pairs, 2, PIX, 2 * PIX), BF16),
        pltpu.VMEM((pairs, PIX, PIX), F32),
        pltpu.VMEM((pairs, PIX, PIX), F32),
    ]


QUARTER = jax.ShapeDtypeStruct((HALF, HALF), F32)
QUARTERS = jax.ShapeDtypeStruct((4, HALF, HALF), F32)
WHOLE_TILE = jax.ShapeDtypeStruct((2, 512, 512), F32)
LOWER = jax.ShapeDtypeStruct((2, PIX, 768), F32)
TOKEN = jax.ShapeDtypeStruct((8, HALF), F32)
BLOCK = jax.ShapeDtypeStruct((2, PIX, PIX), F32)


def process_early(counts, positions, measured, tile, probe, tables):
    pairs = 2
    return pl.pallas_call(
        functools.partial(early_kernel, pairs),
        in_specs=[SMEM] * 2 + [HBM] * 2 + [VMEM] * 2,
        out_specs=[VMEM] * 3,
        out_shape=[
            jax.ShapeDtypeStruct((16, PIX, PIX), F32),
            jax.ShapeDtypeStruct((2, TILES + 1, 512, HALF), F32),
            jax.ShapeDtypeStruct((2, 4, HALF, HALF), F32),
        ],
        scratch_shapes=[
            pltpu.VMEM((16, 2, PIX, HALF), F32),
            pltpu.VMEM((2, TILES + 1, 512, HALF), F32),
            pltpu.SMEM((16,), jnp.int32),
            pltpu.SemaphoreType.DMA((16, 2)),
            pltpu.SemaphoreType.DMA((TILES,)),
        ] + work_shapes(pairs),
        compiler_params=pltpu.CompilerParams(vmem_limit_bytes=26 * 1024 * 1024),
        cost_estimate=pl.CostEstimate(flops=0, bytes_accessed=2**20, transcendentals=0),
        name="early_slots",
    )(counts, positions, measured, tile, probe, tables)


def process_local(counts, positions, tile, lower, held, pacc, ordered, probe, tables):
    pairs = 2
    return pl.pallas_call(
        functools.partial(local_kernel, pairs),
        in_specs=[SMEM] * 2 + [HBM] * 2 + [VMEM] * 5,
        out_specs=[VMEM] * 2,
        out_shape=[jax.ShapeDtypeStruct((2, TILES + 1, 768, HALF), F32), jax.ShapeDtypeStruct((2, 4, HALF, HALF), F32)],
        scratch_shapes=[
            pltpu.VMEM((2, TILES + 1, 768, HALF), F32),
            pltpu.SMEM((16,), jnp.int32),
            pltpu.SemaphoreType.DMA((2 * TILES,)),
        ] + work_shapes(pairs),
        compiler_params=pltpu.CompilerParams(vmem_limit_bytes=26 * 1024 * 1024),
        cost_estimate=pl.CostEstimate(flops=6 * 10**9, bytes_accessed=20 * 2**20, transcendentals=2**20),
        name="local_slots",
    )(counts, positions, tile, lower, held, pacc, ordered, probe, tables)


def process_rest(counts, positions, tile, top, bottom, lower, corner, held, pacc, ordered, probe, tables):
    pairs = 2
    return pl.pallas_call(
        functools.partial(rest_kernel, pairs),
        in_specs=[SMEM] * 2 + [HBM] * 5 + [ANYWHERE] + [VMEM] * 4,
        out_specs=[HBM] + [VMEM] * 5,
        out_shape=[WHOLE_TILE] + [BLOCK] * 2 + [LOWER] + [QUARTERS] * 2,
        scratch_shapes=[
            pltpu.VMEM((2, TILES + 2, 768, HALF), F32),
            pltpu.VMEM((2, TILES + 2, 768, HALF), F32),
            pltpu.VMEM((2, 4, HALF, HALF), F32),
            pltpu.SMEM((16,), jnp.int32),
            pltpu.SemaphoreType.DMA((18,)),
        ] + work_shapes(pairs),
        compiler_params=pltpu.CompilerParams(vmem_limit_bytes=30 * 1024 * 1024),
        cost_estimate=pl.CostEstimate(flops=13 * 10**9, bytes_accessed=20 * 2**20, transcendentals=2**20),
        name="other_slots",
    )(counts, positions, tile, top, bottom, lower, corner, held, pacc, ordered, probe, tables)


def joined(kernel, name, operands, outs, smem=0, beside=()):
    return pl.pallas_call(
        kernel,
        in_specs=[SMEM] * smem + [VMEM] * (len(operands) - smem) + [ANYWHERE] * len(beside),
        out_specs=[VMEM] * len(outs),
        out_shape=list(outs),
        compiler_params=pltpu.CompilerParams(vmem_limit_bytes=16 * 1024 * 1024),
        cost_estimate=pl.CostEstimate(flops=2**18, bytes_accessed=2**20, transcendentals=0),
        name=name,
    )(*operands, *beside)


def pair_kernel(mine_ref, came_ref, *outs):
    for k, out in enumerate(outs):
        out[...] = mine_ref[k] + came_ref[k]


def ring_kernel(own, one, two, three, *rest):
    rest[-1][...] = (own[...] + two[...]) + (one[...] + three[...])


def corner_kernel(own, one, two, three, top, lower, bottom, part, rim):
    ring_kernel(own, one, two, three, part)
    rim[...] = top[...] + lower[:, :, 512:]


def tile_kernel(tile, top, bottom, lower, out, token):
    out[:, :PIX, :PIX] = tile[:, :PIX, :PIX] + (lower[:, :, :PIX] + top[...])
    out[:, :PIX, PIX:] = tile[:, :PIX, PIX:] + lower[:, :, PIX:512]
    out[:, PIX:, :PIX] = tile[:, PIX:, :PIX] + bottom[...]
    out[:, PIX:, PIX:] = tile[:, PIX:, PIX:]
    token[...] = jnp.zeros_like(token)


def half_kernel(own, one, two, three, token, half):
    for k, part in enumerate((own, one, two, three)):
        half[(lax.axis_index("col") // 4 + 4 - k) % 4] = part[...]


def probe_kernel(counts, probe, half, other, out):
    core = lax.axis_index("row") % 2
    root = jnp.sqrt(jnp.sum(counts[...].astype(F32), axis=1, keepdims=True))
    for q in range(4):
        at = (slice(q % 2 * HALF, (q % 2 + 1) * HALF), slice(q // 2 * HALF, (q // 2 + 1) * HALF))
        mine, theirs = half[q], other[q]
        out[(0,) + at] = probe[(0,) + at] + jnp.where(core == 0, mine, theirs) / root
        out[(1,) + at] = probe[(1,) + at] + jnp.where(core == 0, theirs, mine) / root


def passed_along(shard, axis, by):
    peers = lax.axis_size(axis)
    pairs = [(i, i + by) for i in range(peers) if 0 <= i + by < peers]
    return lax.ppermute(shard, axis, pairs)


def over_core(v):
    return lax.ppermute(v, "row", [(i, i ^ 1) for i in range(8)])


def over_x(v, k):
    return lax.ppermute(v, "row", [(i, (i + 2 * k) % 8) for i in range(8)])


def over_y(v, k):
    return lax.ppermute(v, "col", [(i, (i + 4 * k) % 16) for i in range(16)])


def over_z(v, k):
    return lax.ppermute(v, "col", [(i, i // 4 * 4 + (i % 4 + k) % 4) for i in range(16)])


def per_device(object_field, probe_field, measured, positions, counts):
    tables = jnp.asarray(dft_tables())
    top = passed_along(object_field[:, :PIX, :PIX], "col", -1)
    bottom = passed_along(object_field[:, PIX:, :PIX], "col", -1)
    lower = passed_along(object_field[:, :PIX, :], "row", -1)
    corner = passed_along(top, "row", -1)
    where = (counts, positions.T)
    ordered, held, pacc = process_early(*where, measured, object_field, probe_field, tables)
    held, pacc = process_local(*where, object_field, lower, held, pacc, ordered, probe_field, tables)
    tile, top_sum, bottom_sum, lower_sum, mine, other = process_rest(
        *where, object_field, top, bottom, lower, corner, held, pacc, ordered, probe_field, tables
    )
    lower_back = passed_along(lower_sum, "row", 1)
    bottom_back = passed_along(bottom_sum, "col", 1)
    quarters = joined(pair_kernel, "pair_sum", (mine, over_core(other)), [QUARTER] * 4)
    (part,) = joined(
        ring_kernel, "y_sum", [quarters[0]] + [over_y(quarters[k], k) for k in (1, 2, 3)], [QUARTER]
    )
    part, rim = joined(
        corner_kernel, "z_sum", [part] + [over_z(part, k) for k in (1, 2, 3)] + [top_sum, lower_back],
        [QUARTER, BLOCK], beside=[bottom_back],
    )
    top_back = passed_along(rim, "col", 1)
    (part,) = joined(ring_kernel, "x_sum", [part] + [over_x(part, k) for k in (1, 2, 3)], [QUARTER])
    new_object, token = joined(
        tile_kernel, "new_tile", (tile, top_back, bottom_back, lower_back), [WHOLE_TILE, TOKEN]
    )
    (half,) = joined(
        half_kernel, "half", [part] + [over_y(part, k) for k in (1, 2, 3)], [QUARTERS],
        beside=[token],
    )
    (new_probe,) = joined(
        probe_kernel, "new_probe", (counts[None], probe_field, half, over_core(half)), [BLOCK],
    )
    return (new_object, new_probe)


def solution(mesh):
    placed = (
        P(None, "row", "col"),
        P(),
        P(("row", "col"), None, None),
        P(("row", "col"), None),
        P(),
    )
    return jax.shard_map(
        per_device,
        mesh=mesh,
        in_specs=placed,
        out_specs=(P(None, "row", "col"), P()),
        check_vma=False,
    )
```

```python
import functools
import math

import jax
import jax.numpy as jnp
import numpy as np
from jax import lax
from jax.experimental import pallas as pl
from jax.experimental.pallas import tpu as pltpu
from jax.sharding import PartitionSpec as P

FLOOR_SQUARED = 0.25 * 0.25
OBJECT_RATE = 0.5
PIX = 256
HALF = 128
ROWS = 16
F32 = jnp.float32
BF16 = jnp.bfloat16


TILES = 4


def dft_tables():
    freq = np.arange(HALF)[:, None]
    place = np.arange(HALF)[None, :]
    tables = []
    for odd in (0, 1):
        angle = -2.0 * math.pi * (((2 * freq + odd) * place) % PIX) / PIX
        real, imag = np.cos(angle) / 16.0, np.sin(angle) / 16.0
        whole = np.block([[real, -imag], [imag, real]])
        for matrix in (whole, whole.T):
            high = matrix.astype(jnp.bfloat16)
            tables += [high, (matrix - high.astype(np.float64)).astype(jnp.bfloat16)]
    return np.stack(tables)


def split(value):
    high = value.astype(BF16)
    return high, (value - high.astype(F32)).astype(BF16)


def slot_group(group, lane, window_ref, acc_ref, pacc_ref, probe_ref, measured_ref, table_ref, work):
    patch, probe_r, stack, lanes, spec_e, spec_o = work

    for g in group:
        p, turn = g["p"], g["turn"]
        for i in range(HALF // ROWS):
            pieces = {}
            for half in range(2):
                base = half * HALF + i * ROWS
                planes = []
                for plane in range(2):
                    seen = window_ref[plane, pl.ds(g["tile"], 3), pl.ds(g["top"] + base, ROWS), :]
                    window = (jnp.where(lane < turn, seen[2], seen[0]), seen[1])
                    rolled = [
                        pltpu.roll(probe_ref[plane, base : base + ROWS, t * HALF : (t + 1) * HALF], turn, 1)
                        for t in range(2)
                    ]
                    probe = (
                        jnp.where(lane < turn, rolled[1], rolled[0]),
                        jnp.where(lane < turn, rolled[0], rolled[1]),
                    )
                    for t in range(2):
                        at = (p, plane, slice(base, base + ROWS), slice(t * HALF, (t + 1) * HALF))
                        patch[at] = window[t]
                        probe_r[at] = probe[t]
                    planes.append((window, probe))
                for t in range(2):
                    o_re, q_re = planes[0][0][t], planes[0][1][t]
                    o_im, q_im = planes[1][0][t], planes[1][1][t]
                    pieces[half, t] = (q_re * o_re - q_im * o_im, q_re * o_im + q_im * o_re)
            for t in range(2):
                for c in range(2):
                    upper, under = pieces[0, t][c], pieces[1, t][c]
                    for j, value in enumerate((upper + under, upper - under)):
                        high, low = split(value)
                        r = c * HALF + i * ROWS
                        stack[p, j, r : r + ROWS, t * HALF : (t + 1) * HALF] = low
                        stack[p, j, PIX + r : PIX + r + ROWS, t * HALF : (t + 1) * HALF] = high

    def left_product(p, odd, transposed):
        high = table_ref[4 * odd + 2 * transposed]
        low = table_ref[4 * odd + 2 * transposed + 1]
        both = stack[p, odd]
        return jnp.dot(
            jnp.concatenate([high, high, low], axis=1),
            jnp.concatenate([both, both[PIX:]], axis=0),
            preferred_element_type=F32,
        )

    def right_product(p, odd, transposed):
        high = table_ref[4 * odd + 2 * transposed]
        low = table_ref[4 * odd + 2 * transposed + 1]
        both = lanes[p, odd]
        return jnp.dot(
            jnp.concatenate([both, both[:, PIX:]], axis=1),
            jnp.concatenate([high, high, low], axis=0),
            preferred_element_type=F32,
        )

    for g in group:
        p = g["p"]
        spec_e[p] = left_product(p, 0, 0)
        spec_o[p] = left_product(p, 1, 0)
    for g in group:
        p = g["p"]
        for half, source in enumerate((spec_e, spec_o)):
            for i in range(HALF // ROWS):
                r = half * HALF + i * ROWS
                for c in range(2):
                    s = c * HALF + i * ROWS
                    first = source[p, s : s + ROWS, :HALF]
                    second = source[p, s : s + ROWS, HALF:]
                    for j, value in enumerate((first + second, first - second)):
                        high, low = split(value)
                        lanes[p, j, r : r + ROWS, c * HALF : (c + 1) * HALF] = low
                        lanes[p, j, r : r + ROWS, PIX + c * HALF : PIX + (c + 1) * HALF] = high
    for g in group:
        p = g["p"]
        spec_e[p] = right_product(p, 0, 1)
        spec_o[p] = right_product(p, 1, 1)
    for g in group:
        p = g["p"]
        for j, source in enumerate((spec_e, spec_o)):
            for i in range(PIX // ROWS):
                r = i * ROWS
                re = source[p, r : r + ROWS, :HALF]
                im = source[p, r : r + ROWS, HALF:]
                amplitude = measured_ref[g["index"], r : r + ROWS, j * HALF : (j + 1) * HALF]
                factor = amplitude * lax.rsqrt(jnp.maximum(re * re + im * im, FLOOR_SQUARED))
                for c, value in enumerate((re * factor, im * factor)):
                    high, low = split(value)
                    lanes[p, j, r : r + ROWS, c * HALF : (c + 1) * HALF] = low
                    lanes[p, j, r : r + ROWS, PIX + c * HALF : PIX + (c + 1) * HALF] = high
    for g in group:
        p = g["p"]
        spec_e[p] = right_product(p, 0, 0)
        spec_o[p] = right_product(p, 1, 0)
    for g in group:
        p = g["p"]
        for j in range(2):
            for i in range(HALF // ROWS):
                r = j * HALF + i * ROWS
                for c in range(2):
                    first = spec_e[p, r : r + ROWS, c * HALF : (c + 1) * HALF]
                    second = spec_o[p, r : r + ROWS, c * HALF : (c + 1) * HALF]
                    for t, value in enumerate((first + second, first - second)):
                        high, low = split(value)
                        s = c * HALF + i * ROWS
                        stack[p, j, s : s + ROWS, t * HALF : (t + 1) * HALF] = low
                        stack[p, j, PIX + s : PIX + s + ROWS, t * HALF : (t + 1) * HALF] = high
    for g in group:
        p = g["p"]
        spec_e[p] = left_product(p, 0, 1)
        spec_o[p] = left_product(p, 1, 1)
    for g in group:
        p, turn = g["p"], g["turn"]
        back = (HALF - turn) % HALF
        for i in range(HALF // ROWS):
            for half in range(2):
                base = half * HALF + i * ROWS
                rows = slice(base, base + ROWS)
                object_terms, probe_terms = [], []
                for t in range(2):
                    cols = slice(t * HALF, (t + 1) * HALF)
                    o_re, o_im = patch[p, 0, rows, cols], patch[p, 1, rows, cols]
                    q_re, q_im = probe_r[p, 0, rows, cols], probe_r[p, 1, rows, cols]
                    found = []
                    for c in range(2):
                        s = c * HALF + i * ROWS
                        first = spec_e[p, s : s + ROWS, cols]
                        second = spec_o[p, s : s + ROWS, cols]
                        found.append(first + second if half == 0 else first - second)
                    d_re = jnp.where(g["live"], found[0] - (q_re * o_re - q_im * o_im), 0.0)
                    d_im = jnp.where(g["live"], found[1] - (q_re * o_im + q_im * o_re), 0.0)
                    object_terms.append((q_re * d_re + q_im * d_im, q_re * d_im - q_im * d_re))
                    probe_terms.append((o_re * d_re + o_im * d_im, o_re * d_im - o_im * d_re))
                spots = [
                    (plane, pl.ds(g["tile"], 3), pl.ds(g["top"] + base, ROWS), slice(None)) for plane in range(2)
                ]
                held = [acc_ref[spot] for spot in spots]
                for plane in range(2):
                    mixed, pure = object_terms[0][plane], object_terms[1][plane]
                    acc_ref[spots[plane]] = jnp.stack([
                        held[plane][0] + jnp.where(lane < turn, 0.0, mixed),
                        held[plane][1] + pure,
                        held[plane][2] + jnp.where(lane < turn, mixed, 0.0),
                    ])
                for plane in range(2):
                    rolled = [pltpu.roll(probe_terms[t][plane], back, 1) for t in range(2)]
                    part = slice(i * ROWS, (i + 1) * ROWS)
                    pacc_ref[plane, half, part, :] += jnp.where(lane < HALF - turn, rolled[0], rolled[1])
                    pacc_ref[plane, 2 + half, part, :] += jnp.where(lane < HALF - turn, rolled[1], rolled[0])


EARLY = 4


def own_count(counts_ref):
    return counts_ref[lax.axis_index("row") * lax.axis_size("col") + lax.axis_index("col")]


def slot_loop(pairs, stage, counts_ref, positions_ref, order, refs):
    lane = lax.broadcasted_iota(jnp.int32, (ROWS, HALF), 1)
    above, before = lax.axis_index("row") * 512, lax.axis_index("col") * 512

    def enlist(s, carry):
        n, early = carry
        beside = positions_ref[1, s] - before <= PIX
        first = beside & (positions_ref[0, s] - above <= PIX) & (early < EARLY)
        if stage == 0:
            mine = first
        elif stage == 1:
            mine = beside & jnp.logical_not(first)
        else:
            mine = jnp.logical_not(beside)

        @pl.when(mine)
        def _():
            order[n] = s

        return n + mine.astype(jnp.int32), early + first.astype(jnp.int32)

    total, _ = lax.fori_loop(jnp.int32(0), own_count(counts_ref), enlist, (jnp.int32(0), jnp.int32(0)))

    def body(step, carry):
        group = []
        for p in range(pairs):
            place = step * pairs + p
            index = order[jnp.minimum(place, total - 1)]
            top, left = positions_ref[0, index] - above, positions_ref[1, index] - before
            group.append(dict(
                p=p, index=index, live=place < total, top=top, tile=left // HALF, turn=left % HALF,
            ))
        slot_group(group, lane, *refs)
        return carry

    lax.fori_loop(jnp.int32(0), (total + pairs - 1) // pairs, body, jnp.int32(0))


def early_kernel(
    pairs,
    counts_ref, positions_ref, measured_ref, object_ref, probe_ref, table_ref,
    ordered_out, acc_out, pacc_out,
    raw, ext, order, sems, tile_sems, *work,
):
    tiles = [
        pltpu.make_async_copy(object_ref.at[:, :, pl.ds(t * HALF, HALF)], ext.at[:, t], tile_sems.at[t])
        for t in range(TILES)
    ]

    def coming(s, t):
        return pltpu.make_async_copy(measured_ref.at[s, :, pl.ds(t * HALF, HALF)], raw.at[s, t], sems.at[s, t])

    for s in range(16):
        for t in range(2):
            coming(s, t).start()
    for copy in tiles:
        copy.start()
    acc_out[...] = jnp.zeros_like(acc_out)
    pacc_out[...] = jnp.zeros_like(pacc_out)
    lane = lax.broadcasted_iota(jnp.int32, (HALF, HALF), 1)
    first = lane < 64
    even_first = jnp.where(first, 2 * lane, 2 * lane - 127)
    odd_first = jnp.where(first, 2 * lane + 1, 2 * lane - 128)

    def reorder(s, carry):
        for t in range(2):
            coming(s, t).wait()
        for parity in range(2):
            rows = pl.ds(parity, HALF, stride=2)
            left = jnp.take_along_axis(raw[s, 0, rows, :], even_first, axis=1)
            right = jnp.take_along_axis(raw[s, 1, rows, :], odd_first, axis=1)
            out = slice(parity * HALF, (parity + 1) * HALF)
            ordered_out[s, out, :HALF] = jnp.where(first, left, right)
            ordered_out[s, out, HALF:] = pltpu.roll(jnp.where(first, right, left), 64, 1)
        return carry

    def skip(s, carry):
        for t in range(2):
            coming(s, t).wait()
        return carry

    count = own_count(counts_ref)
    lax.fori_loop(jnp.int32(0), count, reorder, jnp.int32(0))
    lax.fori_loop(count, jnp.int32(16), skip, jnp.int32(0))
    for copy in tiles:
        copy.wait()
    slot_loop(
        pairs, 0, counts_ref, positions_ref, order,
        (ext, acc_out, pacc_out, probe_ref, ordered_out, table_ref, work),
    )


def local_kernel(
    pairs,
    counts_ref, positions_ref, object_ref, lower_rim, held_ref, pacc_ref, ordered_ref, probe_ref, table_ref,
    acc_out, pacc_out,
    ext, order, sems, *work,
):
    copies = []
    for t in range(TILES):
        cols = pl.ds(t * HALF, HALF)
        copies.append(pltpu.make_async_copy(object_ref.at[:, :, cols], ext.at[:, t, pl.ds(0, 512)], sems.at[2 * t]))
        copies.append(
            pltpu.make_async_copy(lower_rim.at[:, :, cols], ext.at[:, t, pl.ds(512, PIX)], sems.at[2 * t + 1])
        )
    for copy in copies:
        copy.start()
    acc_out[:, :, 0:512, :] = held_ref[...]
    acc_out[:, :, 512:768, :] = jnp.zeros((2, TILES + 1, PIX, HALF), F32)
    pacc_out[...] = pacc_ref[...]
    for copy in copies:
        copy.wait()
    slot_loop(
        pairs, 1, counts_ref, positions_ref, order,
        (ext, acc_out, pacc_out, probe_ref, ordered_ref, table_ref, work),
    )


def rest_kernel(
    pairs,
    counts_ref, positions_ref, object_ref, top_rim, bottom_rim, lower_rim, corner_rim, held_ref,
    pacc_ref, ordered_ref, probe_ref, table_ref,
    tile_out, top_out, bottom_out, lower_out, mine_out, other_out,
    ext, acc, pacc, order, sems, *work,
):
    copies = []

    def bring(source, target):
        copies.append(pltpu.make_async_copy(source, target, sems.at[len(copies)]))
        copies[-1].start()

    for t in range(TILES):
        cols = pl.ds(t * HALF, HALF)
        bring(object_ref.at[:, :, cols], ext.at[:, t, pl.ds(0, 512)])
        bring(lower_rim.at[:, :, cols], ext.at[:, t, pl.ds(512, PIX)])
        bring(held_ref.at[:, t], acc.at[:, t])
    for t in range(2):
        cols = pl.ds(t * HALF, HALF)
        bring(top_rim.at[:, :, cols], ext.at[:, TILES + t, pl.ds(0, PIX)])
        bring(bottom_rim.at[:, :, cols], ext.at[:, TILES + t, pl.ds(PIX, PIX)])
        bring(corner_rim.at[:, :, cols], ext.at[:, TILES + t, pl.ds(512, PIX)])
    acc[:, TILES:, :, :] = jnp.zeros((2, 2, 768, HALF), F32)
    pacc[...] = pacc_ref[...]
    for copy in copies:
        copy.wait()
    slot_loop(
        pairs, 2, counts_ref, positions_ref, order,
        (ext, acc, pacc, probe_ref, ordered_ref, table_ref, work),
    )
    y_pos, core = lax.axis_index("col") // 4, lax.axis_index("row") % 2
    for k in range(4):
        mine_out[k] = pacc[core, (y_pos + k) % 4]
        other_out[k] = pacc[1 - core, (y_pos + k) % 4]
    leaving = []
    for t in range(TILES):
        ext[:, t, 0:512, :] = ext[:, t, 0:512, :] + OBJECT_RATE * acc[:, t, 0:512, :]
        leaving.append(
            pltpu.make_async_copy(ext.at[:, t, pl.ds(0, 512)], tile_out.at[:, :, pl.ds(t * HALF, HALF)], sems.at[t])
        )
        leaving[-1].start()
    for t in range(TILES + 2):
        lower_out[:, :, t * HALF : (t + 1) * HALF] = OBJECT_RATE * acc[:, t, 512:768, :]
    for t in range(2):
        cols = slice(t * HALF, (t + 1) * HALF)
        top_out[:, :, cols] = OBJECT_RATE * acc[:, TILES + t, 0:PIX, :]
        bottom_out[:, :, cols] = OBJECT_RATE * acc[:, TILES + t, PIX:512, :]
    for copy in leaving:
        copy.wait()


VMEM = pl.BlockSpec(memory_space=pltpu.VMEM)
SMEM = pl.BlockSpec(memory_space=pltpu.SMEM)
ANYWHERE = pl.BlockSpec(memory_space=pl.ANY)
HBM = pl.BlockSpec(memory_space=pltpu.HBM)


def work_shapes(pairs):
    return [
        pltpu.VMEM((pairs, 2, PIX, PIX), F32),
        pltpu.VMEM((pairs, 2, PIX, PIX), F32),
        pltpu.VMEM((pairs, 2, 2 * PIX, PIX), BF16),
        pltpu.VMEM((pairs, 2, PIX, 2 * PIX), BF16),
        pltpu.VMEM((pairs, PIX, PIX), F32),
        pltpu.VMEM((pairs, PIX, PIX), F32),
    ]


QUARTER = jax.ShapeDtypeStruct((HALF, HALF), F32)
QUARTERS = jax.ShapeDtypeStruct((4, HALF, HALF), F32)
WHOLE_TILE = jax.ShapeDtypeStruct((2, 512, 512), F32)
LOWER = jax.ShapeDtypeStruct((2, PIX, 768), F32)
TOKEN = jax.ShapeDtypeStruct((8, HALF), F32)
BLOCK = jax.ShapeDtypeStruct((2, PIX, PIX), F32)


def process_early(counts, positions, measured, tile, probe, tables):
    pairs = 2
    return pl.pallas_call(
        functools.partial(early_kernel, pairs),
        in_specs=[SMEM] * 2 + [HBM] * 2 + [VMEM] * 2,
        out_specs=[VMEM] * 3,
        out_shape=[
            jax.ShapeDtypeStruct((16, PIX, PIX), F32),
            jax.ShapeDtypeStruct((2, TILES + 1, 512, HALF), F32),
            jax.ShapeDtypeStruct((2, 4, HALF, HALF), F32),
        ],
        scratch_shapes=[
            pltpu.VMEM((16, 2, PIX, HALF), F32),
            pltpu.VMEM((2, TILES + 1, 512, HALF), F32),
            pltpu.SMEM((16,), jnp.int32),
            pltpu.SemaphoreType.DMA((16, 2)),
            pltpu.SemaphoreType.DMA((TILES,)),
        ] + work_shapes(pairs),
        compiler_params=pltpu.CompilerParams(vmem_limit_bytes=26 * 1024 * 1024),
        cost_estimate=pl.CostEstimate(flops=0, bytes_accessed=2**20, transcendentals=0),
        name="early_slots",
    )(counts, positions, measured, tile, probe, tables)


def process_local(counts, positions, tile, lower, held, pacc, ordered, probe, tables):
    pairs = 2
    return pl.pallas_call(
        functools.partial(local_kernel, pairs),
        in_specs=[SMEM] * 2 + [HBM] * 2 + [VMEM] * 5,
        out_specs=[VMEM] * 2,
        out_shape=[jax.ShapeDtypeStruct((2, TILES + 1, 768, HALF), F32), jax.ShapeDtypeStruct((2, 4, HALF, HALF), F32)],
        scratch_shapes=[
            pltpu.VMEM((2, TILES + 1, 768, HALF), F32),
            pltpu.SMEM((16,), jnp.int32),
            pltpu.SemaphoreType.DMA((2 * TILES,)),
        ] + work_shapes(pairs),
        compiler_params=pltpu.CompilerParams(vmem_limit_bytes=26 * 1024 * 1024),
        cost_estimate=pl.CostEstimate(flops=6 * 10**9, bytes_accessed=20 * 2**20, transcendentals=2**20),
        name="local_slots",
    )(counts, positions, tile, lower, held, pacc, ordered, probe, tables)


def process_rest(counts, positions, tile, top, bottom, lower, corner, held, pacc, ordered, probe, tables):
    pairs = 2
    return pl.pallas_call(
        functools.partial(rest_kernel, pairs),
        in_specs=[SMEM] * 2 + [HBM] * 5 + [ANYWHERE] + [VMEM] * 4,
        out_specs=[HBM] + [VMEM] * 5,
        out_shape=[WHOLE_TILE] + [BLOCK] * 2 + [LOWER] + [QUARTERS] * 2,
        scratch_shapes=[
            pltpu.VMEM((2, TILES + 2, 768, HALF), F32),
            pltpu.VMEM((2, TILES + 2, 768, HALF), F32),
            pltpu.VMEM((2, 4, HALF, HALF), F32),
            pltpu.SMEM((16,), jnp.int32),
            pltpu.SemaphoreType.DMA((18,)),
        ] + work_shapes(pairs),
        compiler_params=pltpu.CompilerParams(vmem_limit_bytes=30 * 1024 * 1024),
        cost_estimate=pl.CostEstimate(flops=13 * 10**9, bytes_accessed=20 * 2**20, transcendentals=2**20),
        name="other_slots",
    )(counts, positions, tile, top, bottom, lower, corner, held, pacc, ordered, probe, tables)


def joined(kernel, name, operands, outs, smem=0, beside=()):
    return pl.pallas_call(
        kernel,
        in_specs=[SMEM] * smem + [VMEM] * (len(operands) - smem) + [ANYWHERE] * len(beside),
        out_specs=[VMEM] * len(outs),
        out_shape=list(outs),
        compiler_params=pltpu.CompilerParams(vmem_limit_bytes=16 * 1024 * 1024),
        cost_estimate=pl.CostEstimate(flops=2**18, bytes_accessed=2**20, transcendentals=0),
        name=name,
    )(*operands, *beside)


def pair_kernel(mine_ref, came_ref, *outs):
    for k, out in enumerate(outs):
        out[...] = mine_ref[k] + came_ref[k]


def ring_kernel(own, one, two, three, *rest):
    rest[-1][...] = (own[...] + two[...]) + (one[...] + three[...])


def corner_kernel(own, one, two, three, top, lower, bottom, part, rim):
    ring_kernel(own, one, two, three, part)
    rim[...] = top[...] + lower[:, :, 512:]


def tile_kernel(tile, top, bottom, lower, out, token):
    out[:, :PIX, :PIX] = tile[:, :PIX, :PIX] + (lower[:, :, :PIX] + top[...])
    out[:, :PIX, PIX:] = tile[:, :PIX, PIX:] + lower[:, :, PIX:512]
    out[:, PIX:, :PIX] = tile[:, PIX:, :PIX] + bottom[...]
    out[:, PIX:, PIX:] = tile[:, PIX:, PIX:]
    token[...] = jnp.zeros_like(token)


def half_kernel(own, one, two, three, token, half):
    for k, part in enumerate((own, one, two, three)):
        half[(lax.axis_index("col") // 4 + 4 - k) % 4] = part[...]


def probe_kernel(counts, probe, half, other, out):
    core = lax.axis_index("row") % 2
    root = jnp.sqrt(jnp.sum(counts[...].astype(F32), axis=1, keepdims=True))
    for q in range(4):
        at = (slice(q % 2 * HALF, (q % 2 + 1) * HALF), slice(q // 2 * HALF, (q // 2 + 1) * HALF))
        mine, theirs = half[q], other[q]
        out[(0,) + at] = probe[(0,) + at] + jnp.where(core == 0, mine, theirs) / root
        out[(1,) + at] = probe[(1,) + at] + jnp.where(core == 0, theirs, mine) / root


def passed_along(shard, axis, by):
    peers = lax.axis_size(axis)
    return lax.ppermute(shard, axis, [(i, (i + by) % peers) for i in range(peers)])


def over_core(v):
    return lax.ppermute(v, "row", [(i, i ^ 1) for i in range(8)])


def over_x(v, k):
    return lax.ppermute(v, "row", [(i, (i + 2 * k) % 8) for i in range(8)])


def over_y(v, k):
    return lax.ppermute(v, "col", [(i, (i + 4 * k) % 16) for i in range(16)])


def over_z(v, k):
    return lax.ppermute(v, "col", [(i, i // 4 * 4 + (i % 4 + k) % 4) for i in range(16)])


def per_device(object_field, probe_field, measured, positions, counts):
    tables = jnp.asarray(dft_tables())
    top = passed_along(object_field[:, :PIX, :PIX], "col", -1)
    bottom = passed_along(object_field[:, PIX:, :PIX], "col", -1)
    lower = passed_along(object_field[:, :PIX, :], "row", -1)
    corner = passed_along(top, "row", -1)
    where = (counts, positions.T)
    ordered, held, pacc = process_early(*where, measured, object_field, probe_field, tables)
    held, pacc = process_local(*where, object_field, lower, held, pacc, ordered, probe_field, tables)
    tile, top_sum, bottom_sum, lower_sum, mine, other = process_rest(
        *where, object_field, top, bottom, lower, corner, held, pacc, ordered, probe_field, tables
    )
    lower_back = passed_along(lower_sum, "row", 1)
    bottom_back = passed_along(bottom_sum, "col", 1)
    quarters = joined(pair_kernel, "pair_sum", (mine, over_core(other)), [QUARTER] * 4)
    (part,) = joined(
        ring_kernel, "y_sum", [quarters[0]] + [over_y(quarters[k], k) for k in (1, 2, 3)], [QUARTER]
    )
    part, rim = joined(
        corner_kernel, "z_sum", [part] + [over_z(part, k) for k in (1, 2, 3)] + [top_sum, lower_back],
        [QUARTER, BLOCK], beside=[bottom_back],
    )
    top_back = passed_along(rim, "col", 1)
    (part,) = joined(ring_kernel, "x_sum", [part] + [over_x(part, k) for k in (1, 2, 3)], [QUARTER])
    new_object, token = joined(
        tile_kernel, "new_tile", (tile, top_back, bottom_back, lower_back), [WHOLE_TILE, TOKEN]
    )
    (half,) = joined(
        half_kernel, "half", [part] + [over_y(part, k) for k in (1, 2, 3)], [QUARTERS],
        beside=[token],
    )
    (new_probe,) = joined(
        probe_kernel, "new_probe", (counts[None], probe_field, half, over_core(half)), [BLOCK],
    )
    return (new_object, new_probe)


def solution(mesh):
    placed = (
        P(None, "row", "col"),
        P(),
        P(("row", "col"), None, None),
        P(("row", "col"), None),
        P(),
    )
    return jax.shard_map(
        per_device,
        mesh=mesh,
        in_specs=placed,
        out_specs=(P(None, "row", "col"), P()),
        check_vma=False,
    )
```

```python
import functools
import math

import jax
import jax.numpy as jnp
import numpy as np
from jax import lax
from jax.experimental import pallas as pl
from jax.experimental.pallas import tpu as pltpu
from jax.sharding import PartitionSpec as P

FLOOR_SQUARED = 0.25 * 0.25
OBJECT_RATE = 0.5
PIX = 256
HALF = 128
ROWS = 16
F32 = jnp.float32
BF16 = jnp.bfloat16


TILES = 4


def dft_tables():
    freq = np.arange(HALF)[:, None]
    place = np.arange(HALF)[None, :]
    tables = []
    for odd in (0, 1):
        angle = -2.0 * math.pi * (((2 * freq + odd) * place) % PIX) / PIX
        real, imag = np.cos(angle) / 16.0, np.sin(angle) / 16.0
        whole = np.block([[real, -imag], [imag, real]])
        for matrix in (whole, whole.T):
            high = matrix.astype(jnp.bfloat16)
            tables += [high, (matrix - high.astype(np.float64)).astype(jnp.bfloat16)]
    return np.stack(tables)


def split(value):
    high = value.astype(BF16)
    return high, (value - high.astype(F32)).astype(BF16)


def slot_group(group, lane, window_ref, acc_ref, pacc_ref, probe_ref, measured_ref, table_ref, work):
    patch, probe_r, stack, lanes, spec_e, spec_o = work

    for g in group:
        p, turn = g["p"], g["turn"]
        for i in range(HALF // ROWS):
            pieces = {}
            for half in range(2):
                base = half * HALF + i * ROWS
                planes = []
                for plane in range(2):
                    seen = window_ref[plane, pl.ds(g["tile"], 3), pl.ds(g["top"] + base, ROWS), :]
                    window = (jnp.where(lane < turn, seen[2], seen[0]), seen[1])
                    rolled = [
                        pltpu.roll(probe_ref[plane, base : base + ROWS, t * HALF : (t + 1) * HALF], turn, 1)
                        for t in range(2)
                    ]
                    probe = (
                        jnp.where(lane < turn, rolled[1], rolled[0]),
                        jnp.where(lane < turn, rolled[0], rolled[1]),
                    )
                    for t in range(2):
                        at = (p, plane, slice(base, base + ROWS), slice(t * HALF, (t + 1) * HALF))
                        patch[at] = window[t]
                        probe_r[at] = probe[t]
                    planes.append((window, probe))
                for t in range(2):
                    o_re, q_re = planes[0][0][t], planes[0][1][t]
                    o_im, q_im = planes[1][0][t], planes[1][1][t]
                    pieces[half, t] = (q_re * o_re - q_im * o_im, q_re * o_im + q_im * o_re)
            for t in range(2):
                for c in range(2):
                    upper, under = pieces[0, t][c], pieces[1, t][c]
                    for j, value in enumerate((upper + under, upper - under)):
                        high, low = split(value)
                        r = c * HALF + i * ROWS
                        stack[p, j, r : r + ROWS, t * HALF : (t + 1) * HALF] = low
                        stack[p, j, PIX + r : PIX + r + ROWS, t * HALF : (t + 1) * HALF] = high

    def left_product(p, odd, transposed):
        high = table_ref[4 * odd + 2 * transposed]
        low = table_ref[4 * odd + 2 * transposed + 1]
        both = stack[p, odd]
        return jnp.dot(
            jnp.concatenate([high, high, low], axis=1),
            jnp.concatenate([both, both[PIX:]], axis=0),
            preferred_element_type=F32,
        )

    def right_product(p, odd, transposed):
        high = table_ref[4 * odd + 2 * transposed]
        low = table_ref[4 * odd + 2 * transposed + 1]
        both = lanes[p, odd]
        return jnp.dot(
            jnp.concatenate([both, both[:, PIX:]], axis=1),
            jnp.concatenate([high, high, low], axis=0),
            preferred_element_type=F32,
        )

    for g in group:
        p = g["p"]
        spec_e[p] = left_product(p, 0, 0)
        spec_o[p] = left_product(p, 1, 0)
    for g in group:
        p = g["p"]
        for half, source in enumerate((spec_e, spec_o)):
            for i in range(HALF // ROWS):
                r = half * HALF + i * ROWS
                for c in range(2):
                    s = c * HALF + i * ROWS
                    first = source[p, s : s + ROWS, :HALF]
                    second = source[p, s : s + ROWS, HALF:]
                    for j, value in enumerate((first + second, first - second)):
                        high, low = split(value)
                        lanes[p, j, r : r + ROWS, c * HALF : (c + 1) * HALF] = low
                        lanes[p, j, r : r + ROWS, PIX + c * HALF : PIX + (c + 1) * HALF] = high
    for g in group:
        p = g["p"]
        spec_e[p] = right_product(p, 0, 1)
        spec_o[p] = right_product(p, 1, 1)
    for g in group:
        p = g["p"]
        for j, source in enumerate((spec_e, spec_o)):
            for i in range(PIX // ROWS):
                r = i * ROWS
                re = source[p, r : r + ROWS, :HALF]
                im = source[p, r : r + ROWS, HALF:]
                amplitude = measured_ref[g["index"], r : r + ROWS, j * HALF : (j + 1) * HALF]
                factor = amplitude * lax.rsqrt(jnp.maximum(re * re + im * im, FLOOR_SQUARED))
                for c, value in enumerate((re * factor, im * factor)):
                    high, low = split(value)
                    lanes[p, j, r : r + ROWS, c * HALF : (c + 1) * HALF] = low
                    lanes[p, j, r : r + ROWS, PIX + c * HALF : PIX + (c + 1) * HALF] = high
    for g in group:
        p = g["p"]
        spec_e[p] = right_product(p, 0, 0)
        spec_o[p] = right_product(p, 1, 0)
    for g in group:
        p = g["p"]
        for j in range(2):
            for i in range(HALF // ROWS):
                r = j * HALF + i * ROWS
                for c in range(2):
                    first = spec_e[p, r : r + ROWS, c * HALF : (c + 1) * HALF]
                    second = spec_o[p, r : r + ROWS, c * HALF : (c + 1) * HALF]
                    for t, value in enumerate((first + second, first - second)):
                        high, low = split(value)
                        s = c * HALF + i * ROWS
                        stack[p, j, s : s + ROWS, t * HALF : (t + 1) * HALF] = low
                        stack[p, j, PIX + s : PIX + s + ROWS, t * HALF : (t + 1) * HALF] = high
    for g in group:
        p = g["p"]
        spec_e[p] = left_product(p, 0, 1)
        spec_o[p] = left_product(p, 1, 1)
    for g in group:
        p, turn = g["p"], g["turn"]
        back = (HALF - turn) % HALF
        for i in range(HALF // ROWS):
            for half in range(2):
                base = half * HALF + i * ROWS
                rows = slice(base, base + ROWS)
                object_terms, probe_terms = [], []
                for t in range(2):
                    cols = slice(t * HALF, (t + 1) * HALF)
                    o_re, o_im = patch[p, 0, rows, cols], patch[p, 1, rows, cols]
                    q_re, q_im = probe_r[p, 0, rows, cols], probe_r[p, 1, rows, cols]
                    found = []
                    for c in range(2):
                        s = c * HALF + i * ROWS
                        first = spec_e[p, s : s + ROWS, cols]
                        second = spec_o[p, s : s + ROWS, cols]
                        found.append(first + second if half == 0 else first - second)
                    d_re = jnp.where(g["live"], found[0] - (q_re * o_re - q_im * o_im), 0.0)
                    d_im = jnp.where(g["live"], found[1] - (q_re * o_im + q_im * o_re), 0.0)
                    object_terms.append((q_re * d_re + q_im * d_im, q_re * d_im - q_im * d_re))
                    probe_terms.append((o_re * d_re + o_im * d_im, o_re * d_im - o_im * d_re))
                spots = [
                    (plane, pl.ds(g["tile"], 3), pl.ds(g["top"] + base, ROWS), slice(None)) for plane in range(2)
                ]
                held = [acc_ref[spot] for spot in spots]
                for plane in range(2):
                    mixed, pure = object_terms[0][plane], object_terms[1][plane]
                    acc_ref[spots[plane]] = jnp.stack([
                        held[plane][0] + jnp.where(lane < turn, 0.0, mixed),
                        held[plane][1] + pure,
                        held[plane][2] + jnp.where(lane < turn, mixed, 0.0),
                    ])
                for plane in range(2):
                    rolled = [pltpu.roll(probe_terms[t][plane], back, 1) for t in range(2)]
                    part = slice(i * ROWS, (i + 1) * ROWS)
                    pacc_ref[plane, half, part, :] += jnp.where(lane < HALF - turn, rolled[0], rolled[1])
                    pacc_ref[plane, 2 + half, part, :] += jnp.where(lane < HALF - turn, rolled[1], rolled[0])


EARLY = 4


def own_count(counts_ref):
    return counts_ref[lax.axis_index("row") * lax.axis_size("col") + lax.axis_index("col")]


def slot_loop(pairs, stage, counts_ref, positions_ref, order, refs):
    lane = lax.broadcasted_iota(jnp.int32, (ROWS, HALF), 1)
    above, before = lax.axis_index("row") * 512, lax.axis_index("col") * 512

    count = own_count(counts_ref)

    def sides(s):
        beside = positions_ref[1, s] - before <= PIX
        return beside, beside & (positions_ref[0, s] - above <= PIX)

    def tally(s, carry):
        beside, whole = sides(s)
        return carry[0] + beside.astype(jnp.int32), carry[1] + whole.astype(jnp.int32)

    besides, wholes = lax.fori_loop(jnp.int32(0), count, tally, (jnp.int32(0), jnp.int32(0)))
    in_early = jnp.minimum(wholes, EARLY) // pairs * pairs
    in_second = besides - in_early
    in_second = in_second - (in_second % pairs) * ((count - besides) % pairs)

    def enlist(s, carry):
        n, early, second = carry
        beside, whole = sides(s)
        first = whole & (early < in_early)
        later = beside & jnp.logical_not(first)
        now = later & (second < in_second)
        if stage == 0:
            mine = first
        elif stage == 1:
            mine = now
        else:
            mine = jnp.logical_not(first | now)

        @pl.when(mine)
        def _():
            order[n] = s

        return n + mine.astype(jnp.int32), early + first.astype(jnp.int32), second + later.astype(jnp.int32)

    total, _, _ = lax.fori_loop(jnp.int32(0), count, enlist, (jnp.int32(0), jnp.int32(0), jnp.int32(0)))

    def body(step, carry):
        group = []
        for p in range(pairs):
            place = step * pairs + p
            index = order[jnp.minimum(place, total - 1)]
            top, left = positions_ref[0, index] - above, positions_ref[1, index] - before
            group.append(dict(
                p=p, index=index, live=place < total, top=top, tile=left // HALF, turn=left % HALF,
            ))
        slot_group(group, lane, *refs)
        return carry

    lax.fori_loop(jnp.int32(0), (total + pairs - 1) // pairs, body, jnp.int32(0))


def early_kernel(
    pairs,
    counts_ref, positions_ref, measured_ref, object_ref, probe_ref, table_ref,
    ordered_out, acc_out, pacc_out,
    raw, ext, order, sems, tile_sems, *work,
):
    tiles = [
        pltpu.make_async_copy(object_ref.at[:, :, pl.ds(t * HALF, HALF)], ext.at[:, t], tile_sems.at[t])
        for t in range(TILES)
    ]

    def coming(s, t):
        return pltpu.make_async_copy(measured_ref.at[s, :, pl.ds(t * HALF, HALF)], raw.at[s, t], sems.at[s, t])

    for s in range(16):
        for t in range(2):
            coming(s, t).start()
    for copy in tiles:
        copy.start()
    acc_out[...] = jnp.zeros_like(acc_out)
    pacc_out[...] = jnp.zeros_like(pacc_out)
    lane = lax.broadcasted_iota(jnp.int32, (HALF, HALF), 1)
    first = lane < 64
    even_first = jnp.where(first, 2 * lane, 2 * lane - 127)
    odd_first = jnp.where(first, 2 * lane + 1, 2 * lane - 128)

    def reorder(step, carry):
        for s in (2 * step, 2 * step + 1):
            for t in range(2):
                coming(s, t).wait()
        for s in (2 * step, 2 * step + 1):
            for parity in range(2):
                rows = pl.ds(parity, HALF, stride=2)
                left = jnp.take_along_axis(raw[s, 0, rows, :], even_first, axis=1)
                right = jnp.take_along_axis(raw[s, 1, rows, :], odd_first, axis=1)
                out = slice(parity * HALF, (parity + 1) * HALF)
                ordered_out[s, out, :HALF] = jnp.where(first, left, right)
                ordered_out[s, out, HALF:] = pltpu.roll(jnp.where(first, right, left), 64, 1)
        return carry

    def skip(s, carry):
        for t in range(2):
            coming(s, t).wait()
        return carry

    steps = (own_count(counts_ref) + 1) // 2
    lax.fori_loop(jnp.int32(0), steps, reorder, jnp.int32(0))
    lax.fori_loop(2 * steps, jnp.int32(16), skip, jnp.int32(0))
    for copy in tiles:
        copy.wait()
    slot_loop(
        pairs, 0, counts_ref, positions_ref, order,
        (ext, acc_out, pacc_out, probe_ref, ordered_out, table_ref, work),
    )


def local_kernel(
    pairs,
    counts_ref, positions_ref, object_ref, lower_rim, held_ref, pacc_ref, ordered_ref, probe_ref, table_ref,
    acc_out, pacc_out,
    ext, order, sems, *work,
):
    copies = []
    for t in range(TILES):
        cols = pl.ds(t * HALF, HALF)
        copies.append(pltpu.make_async_copy(object_ref.at[:, :, cols], ext.at[:, t, pl.ds(0, 512)], sems.at[2 * t]))
        copies.append(
            pltpu.make_async_copy(lower_rim.at[:, :, cols], ext.at[:, t, pl.ds(512, PIX)], sems.at[2 * t + 1])
        )
    for copy in copies:
        copy.start()
    acc_out[:, :, 0:512, :] = held_ref[...]
    acc_out[:, :, 512:768, :] = jnp.zeros((2, TILES + 1, PIX, HALF), F32)
    pacc_out[...] = pacc_ref[...]
    for copy in copies:
        copy.wait()
    slot_loop(
        pairs, 1, counts_ref, positions_ref, order,
        (ext, acc_out, pacc_out, probe_ref, ordered_ref, table_ref, work),
    )


def rest_kernel(
    pairs,
    counts_ref, positions_ref, object_ref, top_rim, bottom_rim, lower_rim, corner_rim, held_ref,
    pacc_ref, ordered_ref, probe_ref, table_ref,
    tile_out, top_out, bottom_out, lower_out, mine_out, other_out,
    ext, acc, pacc, order, sems, *work,
):
    copies = []

    def bring(source, target):
        copies.append(pltpu.make_async_copy(source, target, sems.at[len(copies)]))
        copies[-1].start()

    for t in range(TILES):
        cols = pl.ds(t * HALF, HALF)
        bring(object_ref.at[:, :, cols], ext.at[:, t, pl.ds(0, 512)])
        bring(lower_rim.at[:, :, cols], ext.at[:, t, pl.ds(512, PIX)])
        bring(held_ref.at[:, t], acc.at[:, t])
    for t in range(2):
        cols = pl.ds(t * HALF, HALF)
        bring(top_rim.at[:, :, cols], ext.at[:, TILES + t, pl.ds(0, PIX)])
        bring(bottom_rim.at[:, :, cols], ext.at[:, TILES + t, pl.ds(PIX, PIX)])
        bring(corner_rim.at[:, :, cols], ext.at[:, TILES + t, pl.ds(512, PIX)])
    acc[:, TILES:, :, :] = jnp.zeros((2, 2, 768, HALF), F32)
    pacc[...] = pacc_ref[...]
    for copy in copies:
        copy.wait()
    slot_loop(
        pairs, 2, counts_ref, positions_ref, order,
        (ext, acc, pacc, probe_ref, ordered_ref, table_ref, work),
    )
    y_pos, core = lax.axis_index("col") // 4, lax.axis_index("row") % 2
    for k in range(4):
        mine_out[k] = pacc[core, (y_pos + k) % 4]
        other_out[k] = pacc[1 - core, (y_pos + k) % 4]
    leaving = []
    for t in range(TILES):
        ext[:, t, 0:512, :] = ext[:, t, 0:512, :] + OBJECT_RATE * acc[:, t, 0:512, :]
        leaving.append(
            pltpu.make_async_copy(ext.at[:, t, pl.ds(0, 512)], tile_out.at[:, :, pl.ds(t * HALF, HALF)], sems.at[t])
        )
        leaving[-1].start()
    for t in range(TILES + 2):
        lower_out[:, :, t * HALF : (t + 1) * HALF] = OBJECT_RATE * acc[:, t, 512:768, :]
    for t in range(2):
        cols = slice(t * HALF, (t + 1) * HALF)
        top_out[:, :, cols] = OBJECT_RATE * acc[:, TILES + t, 0:PIX, :]
        bottom_out[:, :, cols] = OBJECT_RATE * acc[:, TILES + t, PIX:512, :]
    for copy in leaving:
        copy.wait()


VMEM = pl.BlockSpec(memory_space=pltpu.VMEM)
SMEM = pl.BlockSpec(memory_space=pltpu.SMEM)
ANYWHERE = pl.BlockSpec(memory_space=pl.ANY)
HBM = pl.BlockSpec(memory_space=pltpu.HBM)


def work_shapes(pairs):
    return [
        pltpu.VMEM((pairs, 2, PIX, PIX), F32),
        pltpu.VMEM((pairs, 2, PIX, PIX), F32),
        pltpu.VMEM((pairs, 2, 2 * PIX, PIX), BF16),
        pltpu.VMEM((pairs, 2, PIX, 2 * PIX), BF16),
        pltpu.VMEM((pairs, PIX, PIX), F32),
        pltpu.VMEM((pairs, PIX, PIX), F32),
    ]


QUARTER = jax.ShapeDtypeStruct((HALF, HALF), F32)
QUARTERS = jax.ShapeDtypeStruct((4, HALF, HALF), F32)
WHOLE_TILE = jax.ShapeDtypeStruct((2, 512, 512), F32)
LOWER = jax.ShapeDtypeStruct((2, PIX, 768), F32)
TOKEN = jax.ShapeDtypeStruct((8, HALF), F32)
BLOCK = jax.ShapeDtypeStruct((2, PIX, PIX), F32)


def process_early(counts, positions, measured, tile, probe, tables):
    pairs = 2
    return pl.pallas_call(
        functools.partial(early_kernel, pairs),
        in_specs=[SMEM] * 2 + [HBM] * 2 + [VMEM] * 2,
        out_specs=[VMEM] * 3,
        out_shape=[
            jax.ShapeDtypeStruct((16, PIX, PIX), F32),
            jax.ShapeDtypeStruct((2, TILES + 1, 512, HALF), F32),
            jax.ShapeDtypeStruct((2, 4, HALF, HALF), F32),
        ],
        scratch_shapes=[
            pltpu.VMEM((16, 2, PIX, HALF), F32),
            pltpu.VMEM((2, TILES + 1, 512, HALF), F32),
            pltpu.SMEM((16,), jnp.int32),
            pltpu.SemaphoreType.DMA((16, 2)),
            pltpu.SemaphoreType.DMA((TILES,)),
        ] + work_shapes(pairs),
        compiler_params=pltpu.CompilerParams(vmem_limit_bytes=26 * 1024 * 1024),
        cost_estimate=pl.CostEstimate(flops=0, bytes_accessed=2**20, transcendentals=0),
        name="early_slots",
    )(counts, positions, measured, tile, probe, tables)


def process_local(counts, positions, tile, lower, held, pacc, ordered, probe, tables):
    pairs = 2
    return pl.pallas_call(
        functools.partial(local_kernel, pairs),
        in_specs=[SMEM] * 2 + [HBM] * 2 + [VMEM] * 5,
        out_specs=[VMEM] * 2,
        out_shape=[jax.ShapeDtypeStruct((2, TILES + 1, 768, HALF), F32), jax.ShapeDtypeStruct((2, 4, HALF, HALF), F32)],
        scratch_shapes=[
            pltpu.VMEM((2, TILES + 1, 768, HALF), F32),
            pltpu.SMEM((16,), jnp.int32),
            pltpu.SemaphoreType.DMA((2 * TILES,)),
        ] + work_shapes(pairs),
        compiler_params=pltpu.CompilerParams(vmem_limit_bytes=26 * 1024 * 1024),
        cost_estimate=pl.CostEstimate(flops=6 * 10**9, bytes_accessed=20 * 2**20, transcendentals=2**20),
        name="local_slots",
    )(counts, positions, tile, lower, held, pacc, ordered, probe, tables)


def process_rest(counts, positions, tile, top, bottom, lower, corner, held, pacc, ordered, probe, tables):
    pairs = 2
    return pl.pallas_call(
        functools.partial(rest_kernel, pairs),
        in_specs=[SMEM] * 2 + [HBM] * 5 + [ANYWHERE] + [VMEM] * 4,
        out_specs=[HBM] + [VMEM] * 5,
        out_shape=[WHOLE_TILE] + [BLOCK] * 2 + [LOWER] + [QUARTERS] * 2,
        scratch_shapes=[
            pltpu.VMEM((2, TILES + 2, 768, HALF), F32),
            pltpu.VMEM((2, TILES + 2, 768, HALF), F32),
            pltpu.VMEM((2, 4, HALF, HALF), F32),
            pltpu.SMEM((16,), jnp.int32),
            pltpu.SemaphoreType.DMA((18,)),
        ] + work_shapes(pairs),
        compiler_params=pltpu.CompilerParams(vmem_limit_bytes=30 * 1024 * 1024),
        cost_estimate=pl.CostEstimate(flops=13 * 10**9, bytes_accessed=20 * 2**20, transcendentals=2**20),
        name="other_slots",
    )(counts, positions, tile, top, bottom, lower, corner, held, pacc, ordered, probe, tables)


def joined(kernel, name, operands, outs, smem=0, beside=()):
    return pl.pallas_call(
        kernel,
        in_specs=[SMEM] * smem + [VMEM] * (len(operands) - smem) + [ANYWHERE] * len(beside),
        out_specs=[VMEM] * len(outs),
        out_shape=list(outs),
        compiler_params=pltpu.CompilerParams(vmem_limit_bytes=16 * 1024 * 1024),
        cost_estimate=pl.CostEstimate(flops=2**18, bytes_accessed=2**20, transcendentals=0),
        name=name,
    )(*operands, *beside)


def pair_kernel(mine_ref, came_ref, *outs):
    for k, out in enumerate(outs):
        out[...] = mine_ref[k] + came_ref[k]


def ring_kernel(own, one, two, three, *rest):
    rest[-1][...] = (own[...] + two[...]) + (one[...] + three[...])


def corner_kernel(own, one, two, three, top, lower, bottom, part, rim):
    ring_kernel(own, one, two, three, part)
    rim[...] = top[...] + lower[:, :, 512:]


def tile_kernel(tile, top, bottom, lower, half, out, token):
    out[:, :PIX, :PIX] = tile[:, :PIX, :PIX] + (lower[:, :, :PIX] + top[...])
    out[:, :PIX, PIX:] = tile[:, :PIX, PIX:] + lower[:, :, PIX:512]
    out[:, PIX:, :PIX] = tile[:, PIX:, :PIX] + bottom[...]
    out[:, PIX:, PIX:] = tile[:, PIX:, PIX:]
    token[...] = jnp.zeros_like(token)


def half_kernel(own, one, two, three, half):
    for k, part in enumerate((own, one, two, three)):
        half[(lax.axis_index("col") // 4 + 4 - k) % 4] = part[...]


def probe_kernel(counts, probe, half, other, token, out):
    core = lax.axis_index("row") % 2
    root = jnp.sqrt(jnp.sum(counts[...].astype(F32), axis=1, keepdims=True))
    for q in range(4):
        at = (slice(q % 2 * HALF, (q % 2 + 1) * HALF), slice(q // 2 * HALF, (q // 2 + 1) * HALF))
        mine, theirs = half[q], other[q]
        out[(0,) + at] = probe[(0,) + at] + jnp.where(core == 0, mine, theirs) / root
        out[(1,) + at] = probe[(1,) + at] + jnp.where(core == 0, theirs, mine) / root


def passed_along(shard, axis, by):
    peers = lax.axis_size(axis)
    return lax.ppermute(shard, axis, [(i, (i + by) % peers) for i in range(peers)])


def over_core(v):
    return lax.ppermute(v, "row", [(i, i ^ 1) for i in range(8)])


def over_x(v, k):
    return lax.ppermute(v, "row", [(i, (i + 2 * k) % 8) for i in range(8)])


def over_y(v, k):
    return lax.ppermute(v, "col", [(i, (i + 4 * k) % 16) for i in range(16)])


def over_z(v, k):
    return lax.ppermute(v, "col", [(i, i // 4 * 4 + (i % 4 + k) % 4) for i in range(16)])


def per_device(object_field, probe_field, measured, positions, counts):
    tables = jnp.asarray(dft_tables())
    top = passed_along(object_field[:, :PIX, :PIX], "col", -1)
    bottom = passed_along(object_field[:, PIX:, :PIX], "col", -1)
    lower = passed_along(object_field[:, :PIX, :], "row", -1)
    corner = passed_along(top, "row", -1)
    where = (counts, positions.T)
    ordered, held, pacc = process_early(*where, measured, object_field, probe_field, tables)
    held, pacc = process_local(*where, object_field, lower, held, pacc, ordered, probe_field, tables)
    tile, top_sum, bottom_sum, lower_sum, mine, other = process_rest(
        *where, object_field, top, bottom, lower, corner, held, pacc, ordered, probe_field, tables
    )
    lower_back = passed_along(lower_sum, "row", 1)
    bottom_back = passed_along(bottom_sum, "col", 1)
    quarters = joined(pair_kernel, "pair_sum", (mine, over_core(other)), [QUARTER] * 4)
    (part,) = joined(
        ring_kernel, "y_sum", [quarters[0]] + [over_y(quarters[k], k) for k in (1, 2, 3)], [QUARTER]
    )
    part, rim = joined(
        corner_kernel, "z_sum", [part] + [over_z(part, k) for k in (1, 2, 3)] + [top_sum, lower_back],
        [QUARTER, BLOCK], beside=[bottom_back],
    )
    top_back = passed_along(rim, "col", 1)
    (part,) = joined(ring_kernel, "x_sum", [part] + [over_x(part, k) for k in (1, 2, 3)], [QUARTER])
    (half,) = joined(half_kernel, "half", [part] + [over_y(part, k) for k in (1, 2, 3)], [QUARTERS])
    new_object, token = joined(
        tile_kernel, "new_tile", (tile, top_back, bottom_back, lower_back), [WHOLE_TILE, TOKEN], beside=[half]
    )
    (new_probe,) = joined(
        probe_kernel, "new_probe", (counts[None], probe_field, half, over_core(half)), [BLOCK], beside=[token]
    )
    return (new_object, new_probe)


def solution(mesh):
    placed = (
        P(None, "row", "col"),
        P(),
        P(("row", "col"), None, None),
        P(("row", "col"), None),
        P(),
    )
    return jax.shard_map(
        per_device,
        mesh=mesh,
        in_specs=placed,
        out_specs=(P(None, "row", "col"), P()),
        check_vma=False,
    )
```
